32 devices in a mesh: rows: 4 (over z), cols: 8 (over y, x, core).
Axes of the slice: x: 2, y: 2, z: 4, core: 2. Of those that a mesh axis runs over, the one named last changes fastest.
Arguments:
- tile_values: bfloat16 [4, 8, 4, 128, 128], P('rows', 'cols'), may hold values from 0.0009994507 to 0.019897461
- tile_rows: int32 [4, 8, 4], P('rows', 'cols'), may hold values from 0 to 7, as said below
- tile_cols: int32 [4, 8, 4], P('rows', 'cols'), may hold values from 0 to 3, as said below
- live_counts: int32 [4, 8], P('rows', 'cols'), may hold values from 1 to 4, as said below
- test_block: float32 [4096, 512], P('cols'), may hold values from -6 to 6
Outputs:
- y_sample: float32 [4096, 512], P(('rows', 'cols'))
- z_power: float32 [4096, 512], P('cols')
- panel_gram: float32 [4, 512, 512], P('rows')
The draws below stay inside these ranges and needn't reach their ends.
Inputs may be any that keep to these rules, and one draw needn't show every extreme that they name: Within one device the pairs (tile_rows, tile_cols) of its slots are distinct. `tile_cols`: column block of a slot within the device's columns. `live_counts`: some device uses all 4 slots.
All inputs are finite; a program needn't handle non-finite values.
Results may differ from the reference program's by a relative error of at most 0.0003.
Values sent between devices are 32-bit elements; how exact they have to be, the bound alone decides.
A program may use at most 64 MiB of HBM per device.

```python
import math
import jax
import jax.numpy as jnp
from jax import lax

TEST_K = 512
RB_DEV = 8
CB_DEV = 4
NB_DEV = 4
CONTEXTS = 4096
N_ROWS = 4
N_COLS = 8


def slot_positions(key):
    keys = jax.random.split(jax.random.fold_in(key, 11), N_ROWS * N_COLS)
    orders = jax.vmap(lambda single: jax.random.permutation(single, RB_DEV * CB_DEV))(keys)
    return orders[:, :NB_DEV].reshape(N_ROWS, N_COLS, NB_DEV).astype(jnp.int32)


def draw_tile_rows(key, part):
    return (slot_positions(key) // CB_DEV).astype(jnp.int32)


def draw_tile_cols(key, part):
    return (slot_positions(key) % CB_DEV).astype(jnp.int32)


def draw_live_counts(key, part):
    lowest = max(NB_DEV // 4, 1)
    total = N_ROWS * N_COLS
    counts = jax.random.randint(jax.random.fold_in(key, 23), (total,), lowest, NB_DEV + 1)
    picks = jax.random.randint(jax.random.fold_in(key, 29), (2,), 0, total)
    places = jnp.arange(total, dtype=jnp.int32)
    counts = jnp.where(places == picks[0], NB_DEV, counts)
    counts = jnp.where((places == picks[1]) & (picks[1] != picks[0]), lowest, counts)
    return counts.reshape(N_ROWS, N_COLS).astype(jnp.int32)


def levels(key, extent, cuts, smallest, largest):
    level, own = 1.0, jax.random.fold_in(key, 6)
    for position, parts in cuts:
        heights = jnp.exp(jax.random.uniform(jax.random.fold_in(own, position), (parts,), jnp.float32, smallest / len(cuts), largest / len(cuts)))
        level = level * jnp.repeat(heights, extent[position] // parts).reshape([-1 if axis == position else 1 for axis in range(len(extent))])
    return level


def gaussian(rng, dims, width, limit, shards=(), kind=jnp.bfloat16):
    loudness = levels(rng, dims, shards, -0.22, 0.18) if shards else 1.0
    result = jax.random.normal(rng, dims, jnp.float32) * width * loudness
    return jnp.minimum(jnp.maximum(result, -limit), limit).astype(kind)


def setup_inputs(seed: int = 0) -> dict:
    splits = jax.random.split(jax.random.key(seed), 6)
    tile_values = jnp.clip(jnp.exp(math.log(0.019897461) - 2.9911416 * jax.random.uniform(splits[0], (N_ROWS, N_COLS, NB_DEV, 128, 128), jnp.float32) ** levels(splits[0], (N_ROWS, N_COLS, NB_DEV, 128, 128), ((0, 4), (1, 8)), -0.2, 0.2)), 0.0009994507, 0.019897461).astype(jnp.bfloat16)
    tile_rows = draw_tile_rows(jax.random.fold_in(splits[5], 71), 0)
    tile_cols = draw_tile_cols(jax.random.fold_in(splits[5], 71), 0)
    live_counts = draw_live_counts(jax.random.fold_in(splits[5], 71), 0)
    test_block = gaussian(splits[4], (CONTEXTS, TEST_K), 1.0, 6.0, ((0, 8),), jnp.float32)
    return {"tile_values": tile_values, "tile_rows": tile_rows, "tile_cols": tile_cols, "live_counts": live_counts, "test_block": test_block}


def reference(tile_values, tile_rows, tile_cols, live_counts, test_block):
    test_cols = test_block.shape[1]
    omega_tiles = test_block.reshape(N_COLS * CB_DEV, 128, test_cols)
    slot_index = jnp.arange(NB_DEV, dtype=jnp.int32)
    col_base = (CB_DEV * jnp.arange(N_COLS, dtype=jnp.int32))[:, None]
    high = lax.Precision.HIGHEST

    def row_panel(z_total, inputs):
        tile_data, rows_local, cols_local, counts = inputs
        keep_mask = (slot_index[None, :] < counts[:, None]).astype(jnp.float32)
        global_cols = (cols_local + col_base).astype(jnp.int32)
        tiles_f = tile_data.astype(jnp.float32) * keep_mask[:, :, None, None]
        picked = omega_tiles[global_cols]
        products = jnp.einsum("csab,csbk->csak", tiles_f, picked, precision=high)
        onehot = (rows_local[:, :, None] == jnp.arange(RB_DEV, dtype=jnp.int32)[None, None, :]).astype(jnp.float32)
        y_blocks = jnp.einsum("csr,csak->rak", onehot, products, precision=high)
        y_tiles = y_blocks[rows_local]
        z_terms = jnp.einsum("csab,csak->csbk", tiles_f, y_tiles, precision=high)
        z_total = z_total.at[global_cols].add(z_terms)
        y_panel = y_blocks.reshape(RB_DEV * 128, test_cols)
        gram = jnp.dot(y_panel.T, y_panel, precision=high, preferred_element_type=jnp.float32) / (RB_DEV * 128)
        return z_total, (y_panel, gram)

    z_start = jnp.zeros((N_COLS * CB_DEV, 128, test_cols), jnp.float32)
    z_total, outputs = lax.scan(row_panel, z_start, (tile_values, tile_rows, tile_cols, live_counts))
    y_panels, grams = outputs
    y_sample = y_panels.reshape(N_ROWS * RB_DEV * 128, test_cols)
    z_power = z_total.reshape(N_COLS * CB_DEV * 128, test_cols)
    return y_sample, z_power, grams
```

```python
import functools

import jax
import jax.numpy as jnp
from jax import lax
from jax.experimental import pallas as pl
from jax.experimental.pallas import tpu as pltpu
from jax.sharding import PartitionSpec as P

RB_DEV = 8
CB_DEV = 4
B = 128
MESH = pl.DeviceIdType.MESH
F32 = jnp.float32
BF16 = jnp.bfloat16
LAG = 1


def split2(x):
    hi = x.astype(BF16)
    return hi, (x - hi.astype(F32)).astype(BF16)


def kernel(
    n_rows, n_cols, slots,
    rows_ref, cols_ref, live_ref, tiles_ref, om_ref,
    y_out, z_out, g_out,
    codes, sib_codes, tiles_f, sib_tiles, tile_t, sib_om, om2, a_mat, a_t,
    ypart, rs_recv, ypanel, ysib, y2, yhi, ylo, zpart, zin, zcross, ztot,
    init_s, init_r, rs_s, rs_r, ag_s, ag_r, yo_s, yo_r, ys_s, ys_r,
    zc_s, zc_r, zx_r, zt_s, zt_r, zb_s, zf_s,
):
    r = lax.axis_index("rows")
    c = lax.axis_index("cols")
    core = lax.rem(c, 2)
    chip = c // 2
    other = 1 - core
    sib = chip * 2 + other
    m = n_cols // 2
    panel = RB_DEV * B
    ctx = CB_DEV * B
    rpc = panel // m
    half_rows = rpc // 2
    width = om_ref.shape[1] // 2
    chunks = width // B
    pieces = 2 * ctx // B
    mid = n_rows // 2
    lower = r < mid
    inner = jnp.where(lower, r + 1, r - 1)
    outer = jnp.where(lower, r - 1, r + 1)
    is_center = jnp.logical_or(r == mid - 1, r == mid)
    not_center = jnp.logical_not(is_center)
    has_outer = jnp.logical_and(r > 0, r < n_rows - 1)

    def remote(src, dst, ssem, rsem, dev):
        return pltpu.make_async_remote_copy(
            src_ref=src, dst_ref=dst, send_sem=ssem, recv_sem=rsem, device_id=dev, device_id_type=MESH
        )

    barrier = pltpu.get_barrier_semaphore()
    pl.semaphore_signal(barrier, inc=1, device_id=(r, sib), device_id_type=MESH)

    def greet_chip(d, _):
        pl.semaphore_signal(
            barrier, inc=1, device_id=(r, lax.rem(chip + d, m) * 2 + core), device_id_type=MESH
        )
        return 0

    lax.fori_loop(1, m, greet_chip, 0)

    def greet_row(d, _):
        row = lax.rem(r + d, n_rows)
        pl.semaphore_signal(barrier, inc=1, device_id=(row, c), device_id_type=MESH)
        pl.semaphore_signal(barrier, inc=1, device_id=(row, sib), device_id_type=MESH)
        return 0

    lax.fori_loop(1, n_rows, greet_row, 0)

    for s in range(slots):
        code = jnp.where(
            s < live_ref[0, 0], rows_ref[0, 0, s] * CB_DEV + cols_ref[0, 0, s], -1
        )
        codes[s] = jnp.full((8, B), code, jnp.int32)
        tiles_f[s] = tiles_ref[0, 0, s].astype(F32)

    pl.semaphore_wait(barrier, 1 + (m - 1) + 2 * (n_rows - 1))

    init = (
        remote(tiles_f, sib_tiles, init_s.at[0], init_r.at[0], (r, sib)),
        remote(codes, sib_codes, init_s.at[1], init_r.at[1], (r, sib)),
        remote(
            om_ref.at[:, pl.ds(pl.multiple_of(other * width, B), width)],
            sib_om, init_s.at[2], init_r.at[2], (r, sib),
        ),
    )
    for cp in init:
        cp.start()

    def place(code_ref, source, target, row0, col0, rows, cols, row_mul, col_mul):
        def line(i, _):
            for j in range(cols):
                want = i * row_mul + j * col_mul
                val = jnp.zeros((B // 8, 8, B), F32)
                for s in range(slots):
                    hit = jnp.broadcast_to((code_ref[s] == want)[None], val.shape)
                    val = jnp.where(hit, source[s].reshape(val.shape), val)
                target[pl.ds(pl.multiple_of(row0 + i * B, B), B), col0 + j * B : col0 + (j + 1) * B] = (
                    val.reshape(B, B).astype(BF16)
                )
            return 0

        lax.fori_loop(0, rows, line, 0)

    def place_om(src, col0, row0):
        for q in range(chunks):
            hi, lo = split2(src[:, pl.ds(pl.multiple_of(col0 + q * B, B), B)])
            om2[q, row0 : row0 + ctx, 0:B] = hi
            om2[q, row0 : row0 + ctx, B : 2 * B] = lo

    place(codes, tiles_f, a_mat, 0, 0, RB_DEV, CB_DEV, CB_DEV, 1)
    place_om(om_ref, core * width, 0)
    for cp in init:
        cp.wait_recv()
    place(sib_codes, sib_tiles, a_mat, 0, ctx, RB_DEV, CB_DEV, CB_DEV, 1)
    place_om(sib_om, 0, ctx)

    def chip_rows(j):
        return pl.ds(pl.multiple_of(j * rpc, 8), rpc)

    def y_rows(q, j):
        both = jnp.dot(a_mat[chip_rows(j), :], om2[q], preferred_element_type=F32)
        ypart[q, chip_rows(j), :] = both[:, :B] + both[:, B:]

    def rs_copy(q, d):
        j = lax.rem(chip + d, m)
        return remote(
            ypart.at[q, chip_rows(j), :], rs_recv.at[q, d - 1], rs_s.at[q, d - 1], rs_r.at[q, d - 1],
            (r, j * 2 + core),
        )

    def ag_copy(q, d):
        j = lax.rem(chip + d, m)
        mine = ypanel.at[q, chip_rows(chip), :]
        return remote(mine, mine, ag_s.at[q, d - 1], ag_r.at[q, d - 1], (r, j * 2 + core))

    def lanes(q):
        return pl.ds(pl.multiple_of(core * width + q * B, B), B)

    def yo_copy(q):
        return remote(
            ypanel.at[q, pl.ds(pl.multiple_of(chip * rpc + other * half_rows, 8), half_rows), :],
            y_out.at[:, lanes(q)], yo_s.at[q], yo_r.at[q], (r, sib),
        )

    def ys_copy(q):
        return remote(ypanel.at[q], ysib.at[q], ys_s.at[q], ys_r.at[q], (r, sib))

    def each_chip(fn):
        def body(d, _):
            fn(d)
            return 0

        lax.fori_loop(1, m, body, 0)

    def partial_sample(q):
        def send(d):
            y_rows(q, lax.rem(chip + d, m))
            rs_copy(q, d).start()

        each_chip(send)
        y_rows(q, chip)

    def reduce_sample(q):
        each_chip(lambda d: rs_copy(q, d).wait_recv())
        total = ypart[q, chip_rows(chip), :]
        for d in range(m - 1):
            total = total + rs_recv[q, d]
        ypanel[q, chip_rows(chip), :] = total
        each_chip(lambda d: ag_copy(q, d).start())
        yo_copy(q).start()
        y_out[:, lanes(q)] = ypanel[
            q, pl.ds(pl.multiple_of(chip * rpc + core * half_rows, 8), half_rows), :
        ]

    def gather_sample(q):
        each_chip(lambda d: ag_copy(q, d).wait_recv())
        ys_copy(q).start()
        hi, lo = split2(ypanel[q])
        y2[q, :, 0:B] = hi
        y2[q, :, B : 2 * B] = lo
        yhi[:, lanes(q)] = hi
        ylo[:, lanes(q)] = lo

    def piece_rows(i):
        k = i // 2
        start = ctx + k * B if i % 2 == 0 else k * B
        return slice(start, start + B), slice(k * B, (k + 1) * B)

    def inward(q, i, center):
        src, _ = piece_rows(i)
        dst = zcross if center else zin
        sem = zx_r if center else zc_r
        return remote(
            zpart.at[q, src, :], dst.at[q, src, :], zc_s.at[q, i], sem.at[q, i], (inner, c)
        )

    def outward(q, i):
        src, dst = piece_rows(i)
        if i % 2 == 0:
            return remote(
                ztot.at[q, dst, :], z_out.at[dst, lanes(q)], zt_s.at[q, i], zt_r.at[q, i], (outer, sib)
            )
        return remote(
            z_out.at[dst, lanes(q)], z_out.at[dst, lanes(q)], zt_s.at[q, i], zt_r.at[q, i], (outer, c)
        )

    def sideways(q, i):
        _, dst = piece_rows(i)
        return remote(
            ztot.at[q, dst, :], z_out.at[dst, lanes(q)], zb_s.at[q, i // 2], zt_r.at[q, i], (r, sib)
        )

    def other_lanes(q):
        return pl.ds(pl.multiple_of(other * width + q * B, B), B)

    def onward(q, i):
        _, dst = piece_rows(i)
        where = other_lanes(q) if i % 2 == 0 else lanes(q)
        return remote(
            z_out.at[dst, where], z_out.at[dst, where], zf_s.at[q, i], zt_r.at[q, i], (outer, c)
        )

    def finish_piece(q, i):
        src, dst = piece_rows(i)

        @pl.when(is_center)
        def _():
            inward(q, i, True).wait_recv()
            total = zpart[q, src, :] + zcross[q, src, :]
            if i % 2 == 0:
                ztot[q, dst, :] = total
                sideways(q, i).start()
            else:
                z_out[dst, lanes(q)] = total

            @pl.when(has_outer)
            def _():
                outward(q, i).start()

    def chain(q, extra):
        for i in range(pieces):
            src, _ = piece_rows(i)
            both = jnp.dot(a_t[src, :], y2[q], preferred_element_type=F32)
            zpart[q, src, :] = both[:, :B] + both[:, B:]

            @pl.when(has_outer)
            def _():
                inward(q, i, False).wait_recv()
                zpart[q, src, :] += zin[q, src, :]

            @pl.when(is_center)
            def _():
                inward(q, i, True).start()

            @pl.when(not_center)
            def _():
                inward(q, i, False).start()

            if i >= LAG:
                finish_piece(q, i - LAG)
            extra(i)
        for i in range(pieces - LAG, pieces):
            finish_piece(q, i)

    partial_sample(0)
    for s in range(slots):
        tile_t[s] = tiles_f[s].T
    place(codes, tile_t, a_t, 0, 0, CB_DEV, RB_DEV, 1, CB_DEV)
    for s in range(slots):
        tile_t[s] = sib_tiles[s].T
    place(sib_codes, tile_t, a_t, ctx, 0, CB_DEV, RB_DEV, 1, CB_DEV)

    for q in range(chunks):
        if q == 0:
            reduce_sample(0)
        gather_next = q + 1 < chunks
        if gather_next:
            partial_sample(q + 1)
        gather_sample(q)

        def extra(i):
            if gather_next:
                if i == 3:
                    reduce_sample(q + 1)
            else:
                if i == 0:
                    for t in range(chunks):
                        ys_copy(t).wait_recv()
                        hi, lo = split2(ysib[t])
                        yhi[:, other_lanes(t)] = hi
                        ylo[:, other_lanes(t)] = lo
                elif i % 2 == 1 and i // 2 < g_out.shape[1] // B:
                    gram_rows(i // 2)

        def gram_rows(j):
            dims = (((0,), (0,)), ((), ()))
            cols = slice(j * B, (j + 1) * B)
            hi_j, lo_j = yhi[:, cols], ylo[:, cols]
            g = lax.dot_general(hi_j, yhi[...], dims, preferred_element_type=F32)
            g += lax.dot_general(hi_j, ylo[...], dims, preferred_element_type=F32)
            g += lax.dot_general(lo_j, yhi[...], dims, preferred_element_type=F32)
            g_out[0, cols, :] = g * (1.0 / (RB_DEV * B))

        chain(q, extra)

    for q in range(chunks):
        for i in range(pieces):
            if i % 2 == 0:
                outward(q, i).wait_recv()
            else:

                @pl.when(not_center)
                def _():
                    outward(q, i).wait_recv()

            if n_rows > 4:

                @pl.when(jnp.logical_and(has_outer, not_center))
                def _():
                    onward(q, i).start()

    for cp in init:
        cp.wait_send()
    for q in range(chunks):
        each_chip(lambda d: rs_copy(q, d).wait_send())
        each_chip(lambda d: ag_copy(q, d).wait_send())
        yo_copy(q).wait()
        ys_copy(q).wait_send()
        for i in range(pieces):
            inward(q, i, True).wait_send()

            @pl.when(is_center)
            def _():
                if i % 2 == 0:
                    sideways(q, i).wait_send()

                @pl.when(has_outer)
                def _():
                    outward(q, i).wait_send()

            if n_rows > 4:

                @pl.when(jnp.logical_and(has_outer, not_center))
                def _():
                    onward(q, i).wait_send()


def solution(mesh):
    n_rows, n_cols = mesh.shape["rows"], mesh.shape["cols"]

    def local(tile_values, tile_rows, tile_cols, live_counts, test_block):
        slots = tile_values.shape[2]
        test_cols = test_block.shape[1]
        m = n_cols // 2
        panel, ctx = RB_DEV * B, CB_DEV * B
        width = test_cols // 2
        chunks = width // B
        pieces = 2 * ctx // B
        vmem = pl.BlockSpec(memory_space=pltpu.VMEM)
        smem = pl.BlockSpec(memory_space=pltpu.SMEM)
        dma = pltpu.SemaphoreType.DMA
        return pl.pallas_call(
            functools.partial(kernel, n_rows, n_cols, slots),
            out_shape=(
                jax.ShapeDtypeStruct((panel // n_cols, test_cols), F32),
                jax.ShapeDtypeStruct((ctx, test_cols), F32),
                jax.ShapeDtypeStruct((1, test_cols, test_cols), F32),
            ),
            in_specs=[smem, smem, smem, vmem, vmem],
            out_specs=(vmem, vmem, vmem),
            scratch_shapes=[
                pltpu.VMEM((slots, 8, B), jnp.int32),
                pltpu.VMEM((slots, 8, B), jnp.int32),
                pltpu.VMEM((slots, B, B), F32),
                pltpu.VMEM((slots, B, B), F32),
                pltpu.VMEM((slots, B, B), F32),
                pltpu.VMEM((ctx, width), F32),
                pltpu.VMEM((chunks, 2 * ctx, 2 * B), BF16),
                pltpu.VMEM((panel, 2 * ctx), BF16),
                pltpu.VMEM((2 * ctx, panel), BF16),
                pltpu.VMEM((chunks, panel, B), F32),
                pltpu.VMEM((chunks, m - 1, panel // m, B), F32),
                pltpu.VMEM((chunks, panel, B), F32),
                pltpu.VMEM((chunks, panel, B), F32),
                pltpu.VMEM((chunks, panel, 2 * B), BF16),
                pltpu.VMEM((panel, test_cols), BF16),
                pltpu.VMEM((panel, test_cols), BF16),
                pltpu.VMEM((chunks, 2 * ctx, B), F32),
                pltpu.VMEM((chunks, 2 * ctx, B), F32),
                pltpu.VMEM((chunks, 2 * ctx, B), F32),
                pltpu.VMEM((chunks, ctx, B), F32),
                dma((3,)), dma((3,)),
                dma((chunks, m - 1)), dma((chunks, m - 1)),
                dma((chunks, m - 1)), dma((chunks, m - 1)),
                dma((chunks,)), dma((chunks,)),
                dma((chunks,)), dma((chunks,)),
                dma((chunks, pieces)), dma((chunks, pieces)), dma((chunks, pieces)),
                dma((chunks, pieces)), dma((chunks, pieces)),
                dma((chunks, pieces)), dma((chunks, pieces)),
            ],
            compiler_params=pltpu.CompilerParams(
                collective_id=0, has_side_effects=True, vmem_limit_bytes=48 * 1024 * 1024
            ),
            cost_estimate=pl.CostEstimate(flops=4_000_000_000, bytes_accessed=4_000_000, transcendentals=0),
        )(tile_rows, tile_cols, live_counts, tile_values, test_block)

    return jax.shard_map(
        local,
        mesh=mesh,
        in_specs=(
            P("rows", "cols", None, None, None),
            P("rows", "cols", None),
            P("rows", "cols", None),
            P("rows", "cols"),
            P("cols", None),
        ),
        out_specs=(P(("rows", "cols"), None), P("cols", None), P("rows", None, None)),
        check_vma=False,
    )
```

```python
import functools

import jax
import jax.numpy as jnp
from jax import lax
from jax.experimental import pallas as pl
from jax.experimental.pallas import tpu as pltpu
from jax.sharding import PartitionSpec as P

RB_DEV = 8
CB_DEV = 4
B = 128
MESH = pl.DeviceIdType.MESH
F32 = jnp.float32
BF16 = jnp.bfloat16
LAG = 1


def split2(x):
    hi = x.astype(BF16)
    return hi, (x - hi.astype(F32)).astype(BF16)


def kernel(
    n_rows, n_cols, slots,
    rows_ref, cols_ref, live_ref, tiles_ref, om_ref,
    y_out, z_out, g_out,
    codes, sib_codes, tiles_f, sib_tiles, tile_t, sib_om, om2, a_mat, a_t,
    ypart, rs_recv, ypanel, ysib, y2, yhi, ylo, zpart, zin, zcross, ztot,
    init_s, init_r, rs_s, rs_r, ag_s, ag_r, yo_s, yo_r, ys_s, ys_r,
    zc_s, zc_r, zx_r, zt_s, zt_r, zb_s, zf_s, tiles_in, om_in, load_s,
):
    r = lax.axis_index("rows")
    c = lax.axis_index("cols")
    core = lax.rem(c, 2)
    chip = c // 2
    other = 1 - core
    sib = chip * 2 + other
    m = n_cols // 2
    panel = RB_DEV * B
    ctx = CB_DEV * B
    rpc = panel // m
    half_rows = rpc // 2
    width = om_ref.shape[1] // 2
    chunks = width // B
    pieces = 2 * ctx // B
    mid = n_rows // 2
    gram_steps = (1, 3, 5, 6)
    lower = r < mid
    inner = jnp.where(lower, r + 1, r - 1)
    outer = jnp.where(lower, r - 1, r + 1)
    is_center = jnp.logical_or(r == mid - 1, r == mid)
    not_center = jnp.logical_not(is_center)
    has_outer = jnp.logical_and(r > 0, r < n_rows - 1)

    def remote(src, dst, ssem, rsem, dev):
        return pltpu.make_async_remote_copy(
            src_ref=src, dst_ref=dst, send_sem=ssem, recv_sem=rsem, device_id=dev, device_id_type=MESH
        )

    load_tiles = pltpu.make_async_copy(tiles_ref.at[0, 0], tiles_in, load_s.at[0])
    load_om = pltpu.make_async_copy(
        om_ref.at[:, pl.ds(pl.multiple_of(core * width, B), width)], om_in, load_s.at[1]
    )
    load_tiles.start()
    load_om.start()

    barrier = pltpu.get_barrier_semaphore()
    pl.semaphore_signal(barrier, inc=1, device_id=(r, sib), device_id_type=MESH)

    def greet_chip(d, _):
        pl.semaphore_signal(
            barrier, inc=1, device_id=(r, lax.rem(chip + d, m) * 2 + core), device_id_type=MESH
        )
        return 0

    lax.fori_loop(1, m, greet_chip, 0)

    def greet_row(d, _):
        row = lax.rem(r + d, n_rows)
        pl.semaphore_signal(barrier, inc=1, device_id=(row, c), device_id_type=MESH)
        pl.semaphore_signal(barrier, inc=1, device_id=(row, sib), device_id_type=MESH)
        return 0

    lax.fori_loop(1, n_rows, greet_row, 0)

    load_tiles.wait()
    for s in range(slots):
        code = jnp.where(
            s < live_ref[0, 0], rows_ref[0, 0, s] * CB_DEV + cols_ref[0, 0, s], -1
        )
        codes[s] = jnp.full((8, B), code, jnp.int32)
        tiles_f[s] = tiles_in[s].astype(F32)

    pl.semaphore_wait(barrier, 1 + (m - 1) + 2 * (n_rows - 1))

    init = (
        remote(tiles_f, sib_tiles, init_s.at[0], init_r.at[0], (r, sib)),
        remote(codes, sib_codes, init_s.at[1], init_r.at[1], (r, sib)),
        remote(
            om_ref.at[:, pl.ds(pl.multiple_of(other * width, B), width)],
            sib_om, init_s.at[2], init_r.at[2], (r, sib),
        ),
    )
    for cp in init:
        cp.start()

    def place(code_ref, source, target, row0, col0, rows, cols, row_mul, col_mul):
        def line(i, _):
            for j in range(cols):
                want = i * row_mul + j * col_mul
                val = jnp.zeros((B // 8, 8, B), F32)
                for s in range(slots):
                    hit = jnp.broadcast_to((code_ref[s] == want)[None], val.shape)
                    val = jnp.where(hit, source[s].reshape(val.shape), val)
                target[pl.ds(pl.multiple_of(row0 + i * B, B), B), col0 + j * B : col0 + (j + 1) * B] = (
                    val.reshape(B, B).astype(BF16)
                )
            return 0

        lax.fori_loop(0, rows, line, 0)

    def place_om(src, row0):
        for q in range(chunks):
            hi, lo = split2(src[:, q * B : (q + 1) * B])
            om2[q, row0 : row0 + ctx, 0:B] = hi
            om2[q, row0 : row0 + ctx, B : 2 * B] = lo

    place(codes, tiles_f, a_mat, 0, 0, RB_DEV, CB_DEV, CB_DEV, 1)
    load_om.wait()
    place_om(om_in, 0)
    for cp in init:
        cp.wait_recv()
    place(sib_codes, sib_tiles, a_mat, 0, ctx, RB_DEV, CB_DEV, CB_DEV, 1)
    place_om(sib_om, ctx)

    def chip_rows(j):
        return pl.ds(pl.multiple_of(j * rpc, 8), rpc)

    def y_rows(q, j):
        both = jnp.dot(a_mat[chip_rows(j), :], om2[q], preferred_element_type=F32)
        ypart[q, chip_rows(j), :] = both[:, :B] + both[:, B:]

    def rs_copy(q, d):
        j = lax.rem(chip + d, m)
        return remote(
            ypart.at[q, chip_rows(j), :], rs_recv.at[q, d - 1], rs_s.at[q, d - 1], rs_r.at[q, d - 1],
            (r, j * 2 + core),
        )

    def ag_copy(q, d):
        j = lax.rem(chip + d, m)
        mine = ypanel.at[q, chip_rows(chip), :]
        return remote(mine, mine, ag_s.at[q, d - 1], ag_r.at[q, d - 1], (r, j * 2 + core))

    def lanes(q):
        return pl.ds(pl.multiple_of(core * width + q * B, B), B)

    def yo_copy(q):
        return remote(
            ypanel.at[q, pl.ds(pl.multiple_of(chip * rpc + other * half_rows, 8), half_rows), :],
            y_out.at[:, lanes(q)], yo_s.at[q], yo_r.at[q], (r, sib),
        )

    def ys_copy(q):
        return remote(ypanel.at[q], ysib.at[q], ys_s.at[q], ys_r.at[q], (r, sib))

    def each_chip(fn):
        def body(d, _):
            fn(d)
            return 0

        lax.fori_loop(1, m, body, 0)

    def partial_sample(q):
        def send(d):
            y_rows(q, lax.rem(chip + d, m))
            rs_copy(q, d).start()

        each_chip(send)
        y_rows(q, chip)

    def prepare_sample(q):
        each_chip(lambda d: y_rows(q, lax.rem(chip + d, m)))
        y_rows(q, chip)

    def reduce_sample(q):
        each_chip(lambda d: rs_copy(q, d).wait_recv())
        total = ypart[q, chip_rows(chip), :]
        for d in range(m - 1):
            total = total + rs_recv[q, d]
        ypanel[q, chip_rows(chip), :] = total
        each_chip(lambda d: ag_copy(q, d).start())
        yo_copy(q).start()
        y_out[:, lanes(q)] = ypanel[
            q, pl.ds(pl.multiple_of(chip * rpc + core * half_rows, 8), half_rows), :
        ]

    def gather_sample(q, following):
        each_chip(lambda d: ag_copy(q, d).wait_recv())
        if following is not None:
            each_chip(lambda d: rs_copy(following, d).start())
        ys_copy(q).start()
        hi, lo = split2(ypanel[q])
        y2[q, :, 0:B] = hi
        y2[q, :, B : 2 * B] = lo
        yhi[:, lanes(q)] = hi
        ylo[:, lanes(q)] = lo

    def piece_rows(i):
        k = i // 2
        start = ctx + k * B if i % 2 == 0 else k * B
        return slice(start, start + B), slice(k * B, (k + 1) * B)

    def inward(q, i, center):
        src, _ = piece_rows(i)
        dst = zcross if center else zin
        sem = zx_r if center else zc_r
        return remote(
            zpart.at[q, src, :], dst.at[q, src, :], zc_s.at[q, i], sem.at[q, i], (inner, c)
        )

    def outward(q, i):
        src, dst = piece_rows(i)
        if i % 2 == 0:
            return remote(
                ztot.at[q, dst, :], z_out.at[dst, lanes(q)], zt_s.at[q, i], zt_r.at[q, i], (outer, sib)
            )
        return remote(
            z_out.at[dst, lanes(q)], z_out.at[dst, lanes(q)], zt_s.at[q, i], zt_r.at[q, i], (outer, c)
        )

    def sideways(q, i):
        _, dst = piece_rows(i)
        return remote(
            ztot.at[q, dst, :], z_out.at[dst, lanes(q)], zb_s.at[q, i // 2], zt_r.at[q, i], (r, sib)
        )

    def other_lanes(q):
        return pl.ds(pl.multiple_of(other * width + q * B, B), B)

    def onward(q, i):
        _, dst = piece_rows(i)
        where = other_lanes(q) if i % 2 == 0 else lanes(q)
        return remote(
            z_out.at[dst, where], z_out.at[dst, where], zf_s.at[q, i], zt_r.at[q, i], (outer, c)
        )

    def finish_piece(q, i):
        src, dst = piece_rows(i)

        @pl.when(is_center)
        def _():
            inward(q, i, True).wait_recv()
            total = zpart[q, src, :] + zcross[q, src, :]
            if i % 2 == 0:
                ztot[q, dst, :] = total
                sideways(q, i).start()
            else:
                z_out[dst, lanes(q)] = total

            @pl.when(has_outer)
            def _():
                outward(q, i).start()

    def chain(q, extra):
        for i in range(pieces):
            src, _ = piece_rows(i)
            both = jnp.dot(a_t[src, :], y2[q], preferred_element_type=F32)
            zpart[q, src, :] = both[:, :B] + both[:, B:]

            @pl.when(has_outer)
            def _():
                inward(q, i, False).wait_recv()
                zpart[q, src, :] += zin[q, src, :]

            @pl.when(is_center)
            def _():
                inward(q, i, True).start()

            @pl.when(not_center)
            def _():
                inward(q, i, False).start()

            if i >= LAG:
                finish_piece(q, i - LAG)
            extra(i)
        for i in range(pieces - LAG, pieces):
            finish_piece(q, i)

    partial_sample(0)
    for s in range(slots):
        tile_t[s] = tiles_f[s].T
    place(codes, tile_t, a_t, 0, 0, CB_DEV, RB_DEV, 1, CB_DEV)
    for s in range(slots):
        tile_t[s] = sib_tiles[s].T
    place(sib_codes, tile_t, a_t, ctx, 0, CB_DEV, RB_DEV, 1, CB_DEV)

    for q in range(chunks):
        if q == 0:
            reduce_sample(0)
        gather_next = q + 1 < chunks
        if gather_next:
            prepare_sample(q + 1)
        gather_sample(q, q + 1 if gather_next else None)

        def collect_gram():
            for t in range(chunks):
                ys_copy(t).wait_recv()
                hi, lo = split2(ysib[t])
                yhi[:, other_lanes(t)] = hi
                ylo[:, other_lanes(t)] = lo

        def extra(i):
            if gather_next:
                if i == 3:
                    pl.when(is_center)(lambda: reduce_sample(q + 1))
                if i == pieces - 1:
                    pl.when(not_center)(lambda: reduce_sample(q + 1))
                return
            blocks = g_out.shape[1] // B
            if i == 0:
                pl.when(is_center)(collect_gram)
            if i in gram_steps[:blocks]:
                pl.when(is_center)(lambda: gram_rows(gram_steps.index(i)))
            if i == pieces - 1:

                @pl.when(not_center)
                def _():
                    collect_gram()
                    for j in range(blocks):
                        gram_rows(j)

        def gram_rows(j):
            dims = (((0,), (0,)), ((), ()))
            cols = slice(j * B, (j + 1) * B)
            hi_j, lo_j = yhi[:, cols], ylo[:, cols]
            g = lax.dot_general(hi_j, yhi[...], dims, preferred_element_type=F32)
            g += lax.dot_general(hi_j, ylo[...], dims, preferred_element_type=F32)
            g += lax.dot_general(lo_j, yhi[...], dims, preferred_element_type=F32)
            g_out[0, cols, :] = g * (1.0 / (RB_DEV * B))

        chain(q, extra)

    for q in range(chunks):
        for i in range(pieces):
            if i % 2 == 0:
                outward(q, i).wait_recv()
            else:

                @pl.when(not_center)
                def _():
                    outward(q, i).wait_recv()

            if n_rows > 4:

                @pl.when(jnp.logical_and(has_outer, not_center))
                def _():
                    onward(q, i).start()

    for cp in init:
        cp.wait_send()
    for q in range(chunks):
        each_chip(lambda d: rs_copy(q, d).wait_send())
        each_chip(lambda d: ag_copy(q, d).wait_send())
        yo_copy(q).wait()
        ys_copy(q).wait_send()
        for i in range(pieces):
            inward(q, i, True).wait_send()

            @pl.when(is_center)
            def _():
                if i % 2 == 0:
                    sideways(q, i).wait_send()

                @pl.when(has_outer)
                def _():
                    outward(q, i).wait_send()

            if n_rows > 4:

                @pl.when(jnp.logical_and(has_outer, not_center))
                def _():
                    onward(q, i).wait_send()


def solution(mesh):
    n_rows, n_cols = mesh.shape["rows"], mesh.shape["cols"]

    def local(tile_values, tile_rows, tile_cols, live_counts, test_block):
        slots = tile_values.shape[2]
        test_cols = test_block.shape[1]
        m = n_cols // 2
        panel, ctx = RB_DEV * B, CB_DEV * B
        width = test_cols // 2
        chunks = width // B
        pieces = 2 * ctx // B
        vmem = pl.BlockSpec(memory_space=pltpu.VMEM)
        smem = pl.BlockSpec(memory_space=pltpu.SMEM)
        hbm = pl.BlockSpec(memory_space=pl.ANY)
        dma = pltpu.SemaphoreType.DMA
        return pl.pallas_call(
            functools.partial(kernel, n_rows, n_cols, slots),
            out_shape=(
                jax.ShapeDtypeStruct((panel // n_cols, test_cols), F32),
                jax.ShapeDtypeStruct((ctx, test_cols), F32),
                jax.ShapeDtypeStruct((1, test_cols, test_cols), F32),
            ),
            in_specs=[smem, smem, smem, hbm, hbm],
            out_specs=(vmem, vmem, vmem),
            scratch_shapes=[
                pltpu.VMEM((slots, 8, B), jnp.int32),
                pltpu.VMEM((slots, 8, B), jnp.int32),
                pltpu.VMEM((slots, B, B), F32),
                pltpu.VMEM((slots, B, B), F32),
                pltpu.VMEM((slots, B, B), F32),
                pltpu.VMEM((ctx, width), F32),
                pltpu.VMEM((chunks, 2 * ctx, 2 * B), BF16),
                pltpu.VMEM((panel, 2 * ctx), BF16),
                pltpu.VMEM((2 * ctx, panel), BF16),
                pltpu.VMEM((chunks, panel, B), F32),
                pltpu.VMEM((chunks, m - 1, panel // m, B), F32),
                pltpu.VMEM((chunks, panel, B), F32),
                pltpu.VMEM((chunks, panel, B), F32),
                pltpu.VMEM((chunks, panel, 2 * B), BF16),
                pltpu.VMEM((panel, test_cols), BF16),
                pltpu.VMEM((panel, test_cols), BF16),
                pltpu.VMEM((chunks, 2 * ctx, B), F32),
                pltpu.VMEM((chunks, 2 * ctx, B), F32),
                pltpu.VMEM((chunks, 2 * ctx, B), F32),
                pltpu.VMEM((chunks, ctx, B), F32),
                dma((3,)), dma((3,)),
                dma((chunks, m - 1)), dma((chunks, m - 1)),
                dma((chunks, m - 1)), dma((chunks, m - 1)),
                dma((chunks,)), dma((chunks,)),
                dma((chunks,)), dma((chunks,)),
                dma((chunks, pieces)), dma((chunks, pieces)), dma((chunks, pieces)),
                dma((chunks, pieces)), dma((chunks, pieces)),
                dma((chunks, pieces)), dma((chunks, pieces)),
                pltpu.VMEM((slots, B, B), BF16),
                pltpu.VMEM((ctx, width), F32),
                dma((2,)),
            ],
            compiler_params=pltpu.CompilerParams(
                collective_id=0, has_side_effects=True, vmem_limit_bytes=48 * 1024 * 1024
            ),
            cost_estimate=pl.CostEstimate(flops=4_000_000_000, bytes_accessed=4_000_000, transcendentals=0),
        )(tile_rows, tile_cols, live_counts, tile_values, test_block)

    return jax.shard_map(
        local,
        mesh=mesh,
        in_specs=(
            P("rows", "cols", None, None, None),
            P("rows", "cols", None),
            P("rows", "cols", None),
            P("rows", "cols"),
            P("cols", None),
        ),
        out_specs=(P(("rows", "cols"), None), P("cols", None), P("rows", None, None)),
        check_vma=False,
    )
```

```python
import functools

import jax
import jax.numpy as jnp
from jax import lax
from jax.experimental import pallas as pl
from jax.experimental.pallas import tpu as pltpu
from jax.sharding import PartitionSpec as P

RB_DEV = 8
CB_DEV = 4
B = 128
MESH = pl.DeviceIdType.MESH
F32 = jnp.float32
BF16 = jnp.bfloat16
LAG = 1


def split2(x):
    hi = x.astype(BF16)
    return hi, (x - hi.astype(F32)).astype(BF16)


def kernel(
    n_rows, n_cols, slots,
    rows_ref, cols_ref, live_ref, tiles_ref, om_ref,
    y_out, z_out, g_out,
    codes, sib_codes, tiles_in, tiles_f, sib_tiles, tile_t, om_in, sib_om, om2, a_mat, a_t,
    ypart, rs_recv, ypanel, y2, yhi, ylo, zpart, zin, zcross,
    load_s, init_s, init_r, om_s, om_r, rs_s, rs_r, ag_s, ag_r, sb_s, sb_r,
    zc_s, zc_r, zx_r, zt_s, zt_r, zf_s,
):
    r = lax.axis_index("rows")
    c = lax.axis_index("cols")
    core = lax.rem(c, 2)
    chip = c // 2
    other = 1 - core
    sib = chip * 2 + other
    m = n_cols // 2
    panel = RB_DEV * B
    ctx = CB_DEV * B
    share = panel // n_cols
    compact = share == B
    chunks = om_ref.shape[1] // B
    pieces = ctx // B
    mid = n_rows // 2
    lower = r < mid
    inner = jnp.where(lower, r + 1, r - 1)
    outer = jnp.where(lower, r - 1, r + 1)
    is_center = jnp.logical_or(r == mid - 1, r == mid)
    not_center = jnp.logical_not(is_center)
    has_outer = jnp.logical_and(r > 0, r < n_rows - 1)

    def remote(src, dst, ssem, rsem, dev):
        return pltpu.make_async_remote_copy(
            src_ref=src, dst_ref=dst, send_sem=ssem, recv_sem=rsem, device_id=dev, device_id_type=MESH
        )

    def each_chip(fn):
        def body(d, _):
            fn(d)
            return 0

        lax.fori_loop(1, m, body, 0)

    def lanes(q):
        return slice(q * B, (q + 1) * B)

    load_tiles = pltpu.make_async_copy(tiles_ref.at[0, 0], tiles_in, load_s.at[0])
    load_om = [
        pltpu.make_async_copy(om_ref.at[:, lanes(q)], om_in.at[q], load_s.at[1 + q]) for q in range(chunks)
    ]
    load_tiles.start()
    for cp in load_om:
        cp.start()

    barrier = pltpu.get_barrier_semaphore()
    pl.semaphore_signal(barrier, inc=1, device_id=(r, sib), device_id_type=MESH)

    def greet_chip(d):
        pl.semaphore_signal(
            barrier, inc=1, device_id=(r, lax.rem(chip + d, m) * 2 + core), device_id_type=MESH
        )

    each_chip(greet_chip)

    def greet_row(d, _):
        pl.semaphore_signal(barrier, inc=1, device_id=(lax.rem(r + d, n_rows), c), device_id_type=MESH)
        return 0

    lax.fori_loop(1, n_rows, greet_row, 0)

    load_tiles.wait()
    for s in range(slots):
        code = jnp.where(
            s < live_ref[0, 0], rows_ref[0, 0, s] * CB_DEV + cols_ref[0, 0, s], -1
        )
        codes[s] = jnp.full((8, B), code, jnp.int32)
        tiles_f[s] = tiles_in[s].astype(F32)

    pl.semaphore_wait(barrier, 1 + (m - 1) + (n_rows - 1))

    init = (
        remote(tiles_f, sib_tiles, init_s.at[0], init_r.at[0], (r, sib)),
        remote(codes, sib_codes, init_s.at[1], init_r.at[1], (r, sib)),
    )
    om_swap = [
        remote(om_ref.at[:, lanes(q)], sib_om.at[q], om_s.at[q], om_r.at[q], (r, sib)) for q in range(chunks)
    ]
    for cp in (*init, *om_swap):
        cp.start()

    def place(code_ref, source, target, col0, rows, cols, want):
        def line(i, _):
            for j in range(cols):
                code = want(i, j)
                val = jnp.zeros((B // 8, 8, B), F32)
                for s in range(slots):
                    hit = jnp.broadcast_to((code_ref[s] == code)[None], val.shape)
                    val = jnp.where(hit, source[s].reshape(val.shape), val)
                target[pl.ds(pl.multiple_of(i * B, B), B), col0 + j * B : col0 + (j + 1) * B] = (
                    val.reshape(B, B).astype(BF16)
                )
            return 0

        lax.fori_loop(0, rows, line, 0)

    def place_om(q, src, row0):
        hi, lo = split2(src[q])
        om2[q, row0 : row0 + ctx, 0:B] = hi
        om2[q, row0 : row0 + ctx, B : 2 * B] = lo

    if compact:
        a_rows, row_code = m, lambda i, j: (2 * i + core) * CB_DEV + j
    else:
        a_rows, row_code = RB_DEV, lambda i, j: i * CB_DEV + j

    def part_rows(j):
        start = j * share if compact else (2 * j + core) * share
        return pl.ds(pl.multiple_of(start, 8), share)

    def panel_rows(j, parity):
        return pl.ds(pl.multiple_of((2 * j + parity) * share, 8), share)

    def rs_copy(q, d):
        j = lax.rem(chip + d, m)
        return remote(
            ypart.at[q, part_rows(j), :], rs_recv.at[q, d - 1], rs_s.at[q, d - 1], rs_r.at[q, d - 1],
            (r, j * 2 + core),
        )

    def ag_copy(q, d):
        j = lax.rem(chip + d, m)
        mine = ypanel.at[q, panel_rows(chip, core), :]
        return remote(mine, mine, ag_s.at[q, d - 1], ag_r.at[q, d - 1], (r, j * 2 + core))

    def sb_copy(q, d):
        block = ypanel.at[q, panel_rows(lax.rem(chip + m - d, m), core), :]
        return remote(block, block, sb_s.at[q, d], sb_r.at[q, d], (r, sib))

    def partial_sample(q):
        load_om[q].wait()
        place_om(q, om_in, 0)
        om_swap[q].wait_recv()
        place_om(q, sib_om, ctx)
        step = 2 * B
        for k in range(a_rows * B // step):
            rows = slice(k * step, (k + 1) * step)
            both = jnp.dot(a_mat[rows, :], om2[q], preferred_element_type=F32)
            ypart[q, rows, :] = both[:, :B] + both[:, B:]

    def send_sample(q):
        each_chip(lambda d: rs_copy(q, d).start())

    def reduce_sample(q):
        each_chip(lambda d: rs_copy(q, d).wait_recv())
        total = ypart[q, part_rows(chip), :]
        for d in range(m - 1):
            total = total + rs_recv[q, d]
        ypanel[q, panel_rows(chip, core), :] = total
        each_chip(lambda d: ag_copy(q, d).start())
        sb_copy(q, 0).start()
        y_out[:, lanes(q)] = total

    def swap_sample(q):
        def step(d):
            ag_copy(q, d).wait_recv()
            sb_copy(q, d).start()

        each_chip(step)

    def finish_sample(q):
        sb_copy(q, 0).wait_recv()
        each_chip(lambda d: sb_copy(q, d).wait_recv())
        hi, lo = split2(ypanel[q])
        y2[q, :, 0:B] = hi
        y2[q, :, B : 2 * B] = lo
        yhi[:, lanes(q)] = hi
        ylo[:, lanes(q)] = lo

    def gram_rows(q):
        dims = (((0,), (0,)), ((), ()))
        upto = slice(0, (q + 1) * B)
        hi_q, lo_q = yhi[:, lanes(q)], ylo[:, lanes(q)]
        g = lax.dot_general(hi_q, yhi[:, upto], dims, preferred_element_type=F32)
        g += lax.dot_general(hi_q, ylo[:, upto], dims, preferred_element_type=F32)
        g += lax.dot_general(lo_q, yhi[:, upto], dims, preferred_element_type=F32)
        g = g * (1.0 / (RB_DEV * B))
        g_out[0, lanes(q), upto] = g
        for j in range(q):
            g_out[0, lanes(j), lanes(q)] = g[:, lanes(j)].T

    def inward(q, i, center):
        dst = zcross if center else zin
        sem = zx_r if center else zc_r
        return remote(
            zpart.at[q, lanes(i), :], dst.at[q, lanes(i), :], zc_s.at[q, i], sem.at[q, i], (inner, c)
        )

    def outward(q, i):
        piece = z_out.at[lanes(i), lanes(q)]
        return remote(piece, piece, zt_s.at[q, i], zt_r.at[q, i], (outer, c))

    def onward(q, i):
        piece = z_out.at[lanes(i), lanes(q)]
        return remote(piece, piece, zf_s.at[q, i], zt_r.at[q, i], (outer, c))

    def finish_piece(q, i):
        @pl.when(is_center)
        def _():
            inward(q, i, True).wait_recv()
            z_out[lanes(i), lanes(q)] = zpart[q, lanes(i), :] + zcross[q, lanes(i), :]

            @pl.when(has_outer)
            def _():
                outward(q, i).start()

    def chain_piece(q, i):
        both = jnp.dot(a_t[lanes(i), :], y2[q], preferred_element_type=F32)
        zpart[q, lanes(i), :] = both[:, :B] + both[:, B:]

        @pl.when(has_outer)
        def _():
            inward(q, i, False).wait_recv()
            zpart[q, lanes(i), :] += zin[q, lanes(i), :]

        @pl.when(is_center)
        def _():
            inward(q, i, True).start()

        @pl.when(not_center)
        def _():
            inward(q, i, False).start()

    place(codes, tiles_f, a_mat, 0, a_rows, CB_DEV, row_code)
    for cp in init:
        cp.wait_recv()
    place(sib_codes, sib_tiles, a_mat, ctx, a_rows, CB_DEV, row_code)
    partial_sample(0)
    send_sample(0)
    for s in range(slots):
        tile_t[s] = tiles_f[s].T
    place(codes, tile_t, a_t, 0, CB_DEV, RB_DEV, lambda i, j: j * CB_DEV + i)
    if chunks > 1:
        partial_sample(1)
    reduce_sample(0)
    if chunks > 1:
        send_sample(1)
    if chunks > 2:
        partial_sample(2)
    swap_sample(0)
    finish_sample(0)

    late = []
    for q in range(chunks):
        for i in range(pieces):
            chain_piece(q, i)
            late.append((q, i))
            if len(late) > LAG:
                finish_piece(*late.pop(0))
            if i == 0 and q + 1 < chunks:
                reduce_sample(q + 1)
                if q + 2 < chunks:
                    send_sample(q + 2)
            if i == 1:
                gram_rows(q)
                if q + 3 < chunks:
                    partial_sample(q + 3)
            if i == 2 and q + 1 < chunks:
                swap_sample(q + 1)
        if q + 1 < chunks:
            finish_sample(q + 1)
    for item in late:
        finish_piece(*item)

    for q in range(chunks):
        for i in range(pieces):

            @pl.when(not_center)
            def _():
                outward(q, i).wait_recv()

            if n_rows > 4:

                @pl.when(jnp.logical_and(has_outer, not_center))
                def _():
                    onward(q, i).start()

    for cp in (*init, *om_swap):
        cp.wait_send()
    for q in range(chunks):
        each_chip(lambda d: rs_copy(q, d).wait_send())
        each_chip(lambda d: ag_copy(q, d).wait_send())
        sb_copy(q, 0).wait_send()
        each_chip(lambda d: sb_copy(q, d).wait_send())
        for i in range(pieces):
            inward(q, i, True).wait_send()

            @pl.when(jnp.logical_and(is_center, has_outer))
            def _():
                outward(q, i).wait_send()

            if n_rows > 4:

                @pl.when(jnp.logical_and(has_outer, not_center))
                def _():
                    onward(q, i).wait_send()


def solution(mesh):
    n_rows, n_cols = mesh.shape["rows"], mesh.shape["cols"]

    def local(tile_values, tile_rows, tile_cols, live_counts, test_block):
        slots = tile_values.shape[2]
        test_cols = test_block.shape[1]
        m = n_cols // 2
        panel, ctx = RB_DEV * B, CB_DEV * B
        chunks = test_cols // B
        pieces = ctx // B
        share = panel // n_cols
        used = m * B if share == B else panel
        vmem = pl.BlockSpec(memory_space=pltpu.VMEM)
        smem = pl.BlockSpec(memory_space=pltpu.SMEM)
        hbm = pl.BlockSpec(memory_space=pltpu.HBM)
        dma = pltpu.SemaphoreType.DMA
        return pl.pallas_call(
            functools.partial(kernel, n_rows, n_cols, slots),
            out_shape=(
                jax.ShapeDtypeStruct((panel // n_cols, test_cols), F32),
                jax.ShapeDtypeStruct((ctx, test_cols), F32),
                jax.ShapeDtypeStruct((1, test_cols, test_cols), F32),
            ),
            in_specs=[smem, smem, smem, hbm, hbm],
            out_specs=(vmem, vmem, vmem),
            scratch_shapes=[
                pltpu.VMEM((slots, 8, B), jnp.int32),
                pltpu.VMEM((slots, 8, B), jnp.int32),
                pltpu.VMEM((slots, B, B), BF16),
                pltpu.VMEM((slots, B, B), F32),
                pltpu.VMEM((slots, B, B), F32),
                pltpu.VMEM((slots, B, B), F32),
                pltpu.VMEM((chunks, ctx, B), F32),
                pltpu.VMEM((chunks, ctx, B), F32),
                pltpu.VMEM((chunks, 2 * ctx, 2 * B), BF16),
                pltpu.VMEM((used, 2 * ctx), BF16),
                pltpu.VMEM((ctx, panel), BF16),
                pltpu.VMEM((chunks, used, B), F32),
                pltpu.VMEM((chunks, m - 1, share, B), F32),
                pltpu.VMEM((chunks, panel, B), F32),
                pltpu.VMEM((chunks, panel, 2 * B), BF16),
                pltpu.VMEM((panel, test_cols), BF16),
                pltpu.VMEM((panel, test_cols), BF16),
                pltpu.VMEM((chunks, ctx, B), F32),
                pltpu.VMEM((chunks, ctx, B), F32),
                pltpu.VMEM((chunks, ctx, B), F32),
                dma((1 + chunks,)),
                dma((2,)), dma((2,)),
                dma((chunks,)), dma((chunks,)),
                dma((chunks, m - 1)), dma((chunks, m - 1)),
                dma((chunks, m - 1)), dma((chunks, m - 1)),
                dma((chunks, m)), dma((chunks, m)),
                dma((chunks, pieces)), dma((chunks, pieces)), dma((chunks, pieces)),
                dma((chunks, pieces)), dma((chunks, pieces)), dma((chunks, pieces)),
            ],
            compiler_params=pltpu.CompilerParams(
                collective_id=0, has_side_effects=True, vmem_limit_bytes=60 * 1024 * 1024
            ),
            cost_estimate=pl.CostEstimate(flops=4_000_000_000, bytes_accessed=4_000_000, transcendentals=0),
        )(tile_rows, tile_cols, live_counts, tile_values, test_block)

    return jax.shard_map(
        local,
        mesh=mesh,
        in_specs=(
            P("rows", "cols", None, None, None),
            P("rows", "cols", None),
            P("rows", "cols", None),
            P("rows", "cols"),
            P("cols", None),
        ),
        out_specs=(P(("rows", "cols"), None), P("cols", None), P("rows", None, None)),
        check_vma=False,
    )
```

```python
import functools

import jax
import jax.numpy as jnp
from jax import lax
from jax.experimental import pallas as pl
from jax.experimental.pallas import tpu as pltpu
from jax.sharding import PartitionSpec as P

RB_DEV = 8
CB_DEV = 4
B = 128
MESH = pl.DeviceIdType.MESH
F32 = jnp.float32
BF16 = jnp.bfloat16
LAG = 1


def split2(x):
    hi = x.astype(BF16)
    return hi, (x - hi.astype(F32)).astype(BF16)


def kernel(
    n_rows, n_cols, slots,
    rows_ref, cols_ref, live_ref, tiles_ref, om_ref,
    y_out, z_out, g_out,
    codes, sib_codes, tiles_in, tiles_f, sib_tiles, tile_t, om_in, sib_om, om2, a_mat, a_t,
    ypart, rs_recv, ypanel, y2, yhi, ylo, zpart, zin, zcross,
    load_s, init_s, init_r, om_s, om_r, rs_s, rs_r, ag_s, ag_r, sb_s, sb_r,
    zc_s, zc_r, zx_r, zt_s, zt_r, zf_s,
):
    r = lax.axis_index("rows")
    c = lax.axis_index("cols")
    core = lax.rem(c, 2)
    chip = c // 2
    other = 1 - core
    sib = chip * 2 + other
    m = n_cols // 2
    panel = RB_DEV * B
    ctx = CB_DEV * B
    share = panel // n_cols
    compact = share == B
    chunks = om_ref.shape[1] // B
    pieces = ctx // B
    mid = n_rows // 2
    lower = r < mid
    inner = jnp.where(lower, r + 1, r - 1)
    outer = jnp.where(lower, r - 1, r + 1)
    is_center = jnp.logical_or(r == mid - 1, r == mid)
    not_center = jnp.logical_not(is_center)
    has_outer = jnp.logical_and(r > 0, r < n_rows - 1)

    def remote(src, dst, ssem, rsem, dev):
        return pltpu.make_async_remote_copy(
            src_ref=src, dst_ref=dst, send_sem=ssem, recv_sem=rsem, device_id=dev, device_id_type=MESH
        )

    def each_chip(fn):
        def body(d, _):
            fn(d)
            return 0

        lax.fori_loop(1, m, body, 0)

    def lanes(q):
        return slice(q * B, (q + 1) * B)

    load_tiles = pltpu.make_async_copy(tiles_ref.at[0, 0], tiles_in, load_s.at[0])
    load_om = [
        pltpu.make_async_copy(om_ref.at[:, lanes(q)], om_in.at[q], load_s.at[1 + q]) for q in range(chunks)
    ]
    load_tiles.start()
    for cp in load_om:
        cp.start()

    barrier = pltpu.get_barrier_semaphore()
    pl.semaphore_signal(barrier, inc=1, device_id=(r, sib), device_id_type=MESH)

    def greet_chip(d):
        pl.semaphore_signal(
            barrier, inc=1, device_id=(r, lax.rem(chip + d, m) * 2 + core), device_id_type=MESH
        )

    each_chip(greet_chip)

    def greet_row(d, _):
        pl.semaphore_signal(barrier, inc=1, device_id=(lax.rem(r + d, n_rows), c), device_id_type=MESH)
        return 0

    lax.fori_loop(1, n_rows, greet_row, 0)

    load_tiles.wait()
    for s in range(slots):
        code = jnp.where(
            s < live_ref[0, 0], rows_ref[0, 0, s] * CB_DEV + cols_ref[0, 0, s], -1
        )
        codes[s] = jnp.full((8, B), code, jnp.int32)
        tiles_f[s] = tiles_in[s].astype(F32)

    pl.semaphore_wait(barrier, 1 + (m - 1) + (n_rows - 1))

    init = (
        remote(tiles_f, sib_tiles, init_s.at[0], init_r.at[0], (r, sib)),
        remote(codes, sib_codes, init_s.at[1], init_r.at[1], (r, sib)),
    )
    om_swap = [
        remote(om_ref.at[:, lanes(q)], sib_om.at[q], om_s.at[q], om_r.at[q], (r, sib)) for q in range(chunks)
    ]
    for cp in (*init, *om_swap):
        cp.start()

    def place(code_ref, source, target, col0, rows, cols, want):
        def line(i, _):
            for j in range(cols):
                code = want(i, j)
                val = jnp.zeros((B // 8, 8, B), F32)
                for s in range(slots):
                    hit = jnp.broadcast_to((code_ref[s] == code)[None], val.shape)
                    val = jnp.where(hit, source[s].reshape(val.shape), val)
                target[pl.ds(pl.multiple_of(i * B, B), B), col0 + j * B : col0 + (j + 1) * B] = (
                    val.reshape(B, B).astype(BF16)
                )
            return 0

        lax.fori_loop(0, rows, line, 0)

    def place_om(q, src, row0):
        hi, lo = split2(src[q])
        om2[q, row0 : row0 + ctx, 0:B] = hi
        om2[q, row0 : row0 + ctx, B : 2 * B] = lo

    if compact:
        a_rows, row_code = m, lambda i, j: (2 * i + core) * CB_DEV + j
    else:
        a_rows, row_code = RB_DEV, lambda i, j: i * CB_DEV + j

    def part_rows(j):
        start = j * share if compact else (2 * j + core) * share
        return pl.ds(pl.multiple_of(start, 8), share)

    def panel_rows(j, parity):
        return pl.ds(pl.multiple_of((2 * j + parity) * share, 8), share)

    def rs_copy(q, d):
        j = lax.rem(chip + d, m)
        return remote(
            ypart.at[q, part_rows(j), :], rs_recv.at[q, d - 1], rs_s.at[q, d - 1], rs_r.at[q, d - 1],
            (r, j * 2 + core),
        )

    def ag_copy(q, d):
        j = lax.rem(chip + d, m)
        mine = ypanel.at[q, panel_rows(chip, core), :]
        return remote(mine, mine, ag_s.at[q, d - 1], ag_r.at[q, d - 1], (r, j * 2 + core))

    def sb_copy(q, d):
        block = ypanel.at[q, panel_rows(lax.rem(chip + m - d, m), core), :]
        return remote(block, block, sb_s.at[q, d], sb_r.at[q, d], (r, sib))

    def partial_sample(q):
        load_om[q].wait()
        place_om(q, om_in, 0)
        om_swap[q].wait_recv()
        place_om(q, sib_om, ctx)
        step = 2 * B
        for k in range(a_rows * B // step):
            rows = slice(k * step, (k + 1) * step)
            both = jnp.dot(a_mat[rows, :], om2[q], preferred_element_type=F32)
            ypart[q, rows, :] = both[:, :B] + both[:, B:]

    def send_sample(q):
        each_chip(lambda d: rs_copy(q, d).start())

    def reduce_sample(q):
        each_chip(lambda d: rs_copy(q, d).wait_recv())
        total = ypart[q, part_rows(chip), :]
        for d in range(m - 1):
            total = total + rs_recv[q, d]
        ypanel[q, panel_rows(chip, core), :] = total
        each_chip(lambda d: ag_copy(q, d).start())
        sb_copy(q, 0).start()
        y_out[:, lanes(q)] = total

    def swap_sample(q):
        def step(d):
            ag_copy(q, d).wait_recv()
            sb_copy(q, d).start()

        each_chip(step)

    def finish_sample(q):
        sb_copy(q, 0).wait_recv()
        each_chip(lambda d: sb_copy(q, d).wait_recv())
        hi, lo = split2(ypanel[q])
        y2[q, :, 0:B] = hi
        y2[q, :, B : 2 * B] = lo
        yhi[:, lanes(q)] = hi
        ylo[:, lanes(q)] = lo

    def gram_rows(q):
        dims = (((0,), (0,)), ((), ()))
        upto = slice(0, (q + 1) * B)
        hi_q, lo_q = yhi[:, lanes(q)], ylo[:, lanes(q)]
        g = lax.dot_general(hi_q, yhi[:, upto], dims, preferred_element_type=F32)
        g += lax.dot_general(hi_q, ylo[:, upto], dims, preferred_element_type=F32)
        g += lax.dot_general(lo_q, yhi[:, upto], dims, preferred_element_type=F32)
        g = g * (1.0 / (RB_DEV * B))
        g_out[0, lanes(q), upto] = g
        for j in range(q):
            g_out[0, lanes(j), lanes(q)] = g[:, lanes(j)].T

    def inward(q, i, center):
        dst = zcross if center else zin
        sem = zx_r if center else zc_r
        return remote(
            zpart.at[q, lanes(i), :], dst.at[q, lanes(i), :], zc_s.at[q, i], sem.at[q, i], (inner, c)
        )

    def outward(q, i):
        piece = z_out.at[lanes(i), lanes(q)]
        return remote(piece, piece, zt_s.at[q, i], zt_r.at[q, i], (outer, c))

    def onward(q, i):
        piece = z_out.at[lanes(i), lanes(q)]
        return remote(piece, piece, zf_s.at[q, i], zt_r.at[q, i], (outer, c))

    def finish_piece(q, i):
        @pl.when(is_center)
        def _():
            inward(q, i, True).wait_recv()
            z_out[lanes(i), lanes(q)] = zpart[q, lanes(i), :] + zcross[q, lanes(i), :]

            @pl.when(has_outer)
            def _():
                outward(q, i).start()

    def chain_piece(q, i):
        both = jnp.dot(a_t[lanes(i), :], y2[q], preferred_element_type=F32)
        zpart[q, lanes(i), :] = both[:, :B] + both[:, B:]

        @pl.when(has_outer)
        def _():
            inward(q, i, False).wait_recv()
            zpart[q, lanes(i), :] += zin[q, lanes(i), :]

        @pl.when(is_center)
        def _():
            inward(q, i, True).start()

        @pl.when(not_center)
        def _():
            inward(q, i, False).start()

    place(codes, tiles_f, a_mat, 0, a_rows, CB_DEV, row_code)
    for cp in init:
        cp.wait_recv()
    place(sib_codes, sib_tiles, a_mat, ctx, a_rows, CB_DEV, row_code)
    partial_sample(0)
    send_sample(0)
    partial_sample(1)
    send_sample(1)
    for s in range(slots):
        tile_t[s] = tiles_f[s].T
    place(codes, tile_t, a_t, 0, CB_DEV, RB_DEV, lambda i, j: j * CB_DEV + i)
    reduce_sample(0)
    partial_sample(2)
    send_sample(2)
    reduce_sample(1)
    partial_sample(3)
    send_sample(3)
    swap_sample(0)
    finish_sample(0)

    between = {
        (0, 1): lambda: reduce_sample(2),
        (0, 2): lambda: swap_sample(1),
        (0, 3): lambda: (reduce_sample(3), finish_sample(1)),
        (1, 0): lambda: gram_rows(0),
        (1, 1): lambda: swap_sample(2),
        (1, 2): lambda: gram_rows(1),
        (1, 3): lambda: finish_sample(2),
        (2, 0): lambda: swap_sample(3),
        (2, 1): lambda: gram_rows(2),
        (2, 3): lambda: finish_sample(3),
        (3, 1): lambda: gram_rows(3),
    }
    late = []
    for q in range(chunks):
        for i in range(pieces):
            chain_piece(q, i)
            late.append((q, i))
            if len(late) > LAG:
                finish_piece(*late.pop(0))
            if (q, i) in between:
                between[q, i]()
    for item in late:
        finish_piece(*item)

    for q in range(chunks):
        for i in range(pieces):

            @pl.when(not_center)
            def _():
                outward(q, i).wait_recv()

            if n_rows > 4:

                @pl.when(jnp.logical_and(has_outer, not_center))
                def _():
                    onward(q, i).start()

    for cp in (*init, *om_swap):
        cp.wait_send()
    for q in range(chunks):
        each_chip(lambda d: rs_copy(q, d).wait_send())
        each_chip(lambda d: ag_copy(q, d).wait_send())
        sb_copy(q, 0).wait_send()
        each_chip(lambda d: sb_copy(q, d).wait_send())
        for i in range(pieces):
            inward(q, i, True).wait_send()

            @pl.when(jnp.logical_and(is_center, has_outer))
            def _():
                outward(q, i).wait_send()

            if n_rows > 4:

                @pl.when(jnp.logical_and(has_outer, not_center))
                def _():
                    onward(q, i).wait_send()


def solution(mesh):
    n_rows, n_cols = mesh.shape["rows"], mesh.shape["cols"]

    def local(tile_values, tile_rows, tile_cols, live_counts, test_block):
        slots = tile_values.shape[2]
        test_cols = test_block.shape[1]
        m = n_cols // 2
        panel, ctx = RB_DEV * B, CB_DEV * B
        chunks = test_cols // B
        pieces = ctx // B
        share = panel // n_cols
        used = m * B if share == B else panel
        vmem = pl.BlockSpec(memory_space=pltpu.VMEM)
        smem = pl.BlockSpec(memory_space=pltpu.SMEM)
        hbm = pl.BlockSpec(memory_space=pltpu.HBM)
        dma = pltpu.SemaphoreType.DMA
        return pl.pallas_call(
            functools.partial(kernel, n_rows, n_cols, slots),
            out_shape=(
                jax.ShapeDtypeStruct((panel // n_cols, test_cols), F32),
                jax.ShapeDtypeStruct((ctx, test_cols), F32),
                jax.ShapeDtypeStruct((1, test_cols, test_cols), F32),
            ),
            in_specs=[smem, smem, smem, hbm, hbm],
            out_specs=(vmem, vmem, vmem),
            scratch_shapes=[
                pltpu.VMEM((slots, 8, B), jnp.int32),
                pltpu.VMEM((slots, 8, B), jnp.int32),
                pltpu.VMEM((slots, B, B), BF16),
                pltpu.VMEM((slots, B, B), F32),
                pltpu.VMEM((slots, B, B), F32),
                pltpu.VMEM((slots, B, B), F32),
                pltpu.VMEM((chunks, ctx, B), F32),
                pltpu.VMEM((chunks, ctx, B), F32),
                pltpu.VMEM((chunks, 2 * ctx, 2 * B), BF16),
                pltpu.VMEM((used, 2 * ctx), BF16),
                pltpu.VMEM((ctx, panel), BF16),
                pltpu.VMEM((chunks, used, B), F32),
                pltpu.VMEM((chunks, m - 1, share, B), F32),
                pltpu.VMEM((chunks, panel, B), F32),
                pltpu.VMEM((chunks, panel, 2 * B), BF16),
                pltpu.VMEM((panel, test_cols), BF16),
                pltpu.VMEM((panel, test_cols), BF16),
                pltpu.VMEM((chunks, ctx, B), F32),
                pltpu.VMEM((chunks, ctx, B), F32),
                pltpu.VMEM((chunks, ctx, B), F32),
                dma((1 + chunks,)),
                dma((2,)), dma((2,)),
                dma((chunks,)), dma((chunks,)),
                dma((chunks, m - 1)), dma((chunks, m - 1)),
                dma((chunks, m - 1)), dma((chunks, m - 1)),
                dma((chunks, m)), dma((chunks, m)),
                dma((chunks, pieces)), dma((chunks, pieces)), dma((chunks, pieces)),
                dma((chunks, pieces)), dma((chunks, pieces)), dma((chunks, pieces)),
            ],
            compiler_params=pltpu.CompilerParams(
                collective_id=0, has_side_effects=True, vmem_limit_bytes=60 * 1024 * 1024
            ),
            cost_estimate=pl.CostEstimate(flops=4_000_000_000, bytes_accessed=4_000_000, transcendentals=0),
        )(tile_rows, tile_cols, live_counts, tile_values, test_block)

    return jax.shard_map(
        local,
        mesh=mesh,
        in_specs=(
            P("rows", "cols", None, None, None),
            P("rows", "cols", None),
            P("rows", "cols", None),
            P("rows", "cols"),
            P("cols", None),
        ),
        out_specs=(P(("rows", "cols"), None), P("cols", None), P("rows", None, None)),
        check_vma=False,
    )
```

```python
import functools

import jax
import jax.numpy as jnp
from jax import lax
from jax.experimental import pallas as pl
from jax.experimental.pallas import tpu as pltpu
from jax.sharding import PartitionSpec as P

RB_DEV = 8
CB_DEV = 4
B = 128
MESH = pl.DeviceIdType.MESH
F32 = jnp.float32
BF16 = jnp.bfloat16
LAG = 5
PIECE = 64


def split2(x):
    hi = x.astype(BF16)
    return hi, (x - hi.astype(F32)).astype(BF16)


def kernel(
    n_rows, n_cols, slots,
    rows_ref, cols_ref, live_ref, tiles_ref, om_ref,
    y_out, z_out, g_out,
    codes, sib_codes, tiles_in, tiles_f, sib_tiles, tile_t, om_in, sib_om, om2, a_mat, a_t,
    ypart, rs_recv, ypanel, y2, yhi, ylo, zpart, zin, zcross,
    load_s, init_s, init_r, om_s, om_r, rs_s, rs_r, ag_s, ag_r, sb_s, sb_r,
    zc_s, zc_r, zx_r, zt_s, zt_r, zf_s,
):
    r = lax.axis_index("rows")
    c = lax.axis_index("cols")
    core = lax.rem(c, 2)
    chip = c // 2
    other = 1 - core
    sib = chip * 2 + other
    m = n_cols // 2
    panel = RB_DEV * B
    ctx = CB_DEV * B
    share = panel // n_cols
    compact = share == B
    chunks = om_ref.shape[1] // B
    pieces = ctx // PIECE
    mid = n_rows // 2
    lower = r < mid
    inner = jnp.where(lower, r + 1, r - 1)
    outer = jnp.where(lower, r - 1, r + 1)
    is_center = jnp.logical_or(r == mid - 1, r == mid)
    not_center = jnp.logical_not(is_center)
    has_outer = jnp.logical_and(r > 0, r < n_rows - 1)

    def remote(src, dst, ssem, rsem, dev):
        return pltpu.make_async_remote_copy(
            src_ref=src, dst_ref=dst, send_sem=ssem, recv_sem=rsem, device_id=dev, device_id_type=MESH
        )

    def each_chip(fn):
        def body(d, _):
            fn(d)
            return 0

        lax.fori_loop(1, m, body, 0)

    def lanes(q):
        return slice(q * B, (q + 1) * B)

    load_tiles = pltpu.make_async_copy(tiles_ref.at[0, 0], tiles_in, load_s.at[0])
    load_om = [
        pltpu.make_async_copy(om_ref.at[:, lanes(q)], om_in.at[q], load_s.at[1 + q]) for q in range(chunks)
    ]
    load_tiles.start()
    for cp in load_om:
        cp.start()

    barrier = pltpu.get_barrier_semaphore()
    pl.semaphore_signal(barrier, inc=1, device_id=(r, sib), device_id_type=MESH)

    def greet_chip(d):
        pl.semaphore_signal(
            barrier, inc=1, device_id=(r, lax.rem(chip + d, m) * 2 + core), device_id_type=MESH
        )

    each_chip(greet_chip)

    def greet_row(d, _):
        pl.semaphore_signal(barrier, inc=1, device_id=(lax.rem(r + d, n_rows), c), device_id_type=MESH)
        return 0

    lax.fori_loop(1, n_rows, greet_row, 0)

    load_tiles.wait()
    for s in range(slots):
        code = jnp.where(
            s < live_ref[0, 0], rows_ref[0, 0, s] * CB_DEV + cols_ref[0, 0, s], -1
        )
        codes[s] = jnp.full((8, B), code, jnp.int32)
        tiles_f[s] = tiles_in[s].astype(F32)

    pl.semaphore_wait(barrier, 1 + (m - 1) + (n_rows - 1))

    init = (
        remote(tiles_f, sib_tiles, init_s.at[0], init_r.at[0], (r, sib)),
        remote(codes, sib_codes, init_s.at[1], init_r.at[1], (r, sib)),
    )
    om_swap = [
        remote(om_ref.at[:, lanes(q)], sib_om.at[q], om_s.at[q], om_r.at[q], (r, sib)) for q in range(chunks)
    ]
    for cp in (*init, *om_swap):
        cp.start()

    def place(code_ref, source, target, col0, rows, cols, want):
        def line(i, _):
            for j in range(cols):
                code = want(i, j)
                val = jnp.zeros((B // 8, 8, B), F32)
                for s in range(slots):
                    hit = jnp.broadcast_to((code_ref[s] == code)[None], val.shape)
                    val = jnp.where(hit, source[s].reshape(val.shape), val)
                target[pl.ds(pl.multiple_of(i * B, B), B), col0 + j * B : col0 + (j + 1) * B] = (
                    val.reshape(B, B).astype(BF16)
                )
            return 0

        lax.fori_loop(0, rows, line, 0)

    def place_om(q, src, row0):
        hi, lo = split2(src[q])
        om2[q, row0 : row0 + ctx, 0:B] = hi
        om2[q, row0 : row0 + ctx, B : 2 * B] = lo

    if compact:
        a_rows, row_code = m, lambda i, j: (2 * i + core) * CB_DEV + j
    else:
        a_rows, row_code = RB_DEV, lambda i, j: i * CB_DEV + j

    def part_rows(j):
        start = j * share if compact else (2 * j + core) * share
        return pl.ds(pl.multiple_of(start, 8), share)

    def panel_rows(j, parity):
        return pl.ds(pl.multiple_of((2 * j + parity) * share, 8), share)

    def rs_copy(q, d):
        j = lax.rem(chip + d, m)
        return remote(
            ypart.at[q, part_rows(j), :], rs_recv.at[q, d - 1], rs_s.at[q, d - 1], rs_r.at[q, d - 1],
            (r, j * 2 + core),
        )

    def ag_copy(q, d):
        j = lax.rem(chip + d, m)
        mine = ypanel.at[q, panel_rows(chip, core), :]
        return remote(mine, mine, ag_s.at[q, d - 1], ag_r.at[q, d - 1], (r, j * 2 + core))

    def sb_copy(q, d):
        block = ypanel.at[q, panel_rows(lax.rem(chip + m - d, m), core), :]
        return remote(block, block, sb_s.at[q, d], sb_r.at[q, d], (r, sib))

    def partial_sample(q):
        load_om[q].wait()
        place_om(q, om_in, 0)
        om_swap[q].wait_recv()
        place_om(q, sib_om, ctx)
        step = 2 * B
        for k in range(a_rows * B // step):
            rows = slice(k * step, (k + 1) * step)
            both = jnp.dot(a_mat[rows, :], om2[q], preferred_element_type=F32)
            ypart[q, rows, :] = both[:, :B] + both[:, B:]

    def send_sample(q):
        each_chip(lambda d: rs_copy(q, d).start())

    def reduce_sample(q):
        each_chip(lambda d: rs_copy(q, d).wait_recv())
        total = ypart[q, part_rows(chip), :]
        for d in range(m - 1):
            total = total + rs_recv[q, d]
        ypanel[q, panel_rows(chip, core), :] = total
        each_chip(lambda d: ag_copy(q, d).start())
        sb_copy(q, 0).start()
        y_out[:, lanes(q)] = total

    def swap_sample(q):
        def step(d):
            ag_copy(q, d).wait_recv()
            sb_copy(q, d).start()

        each_chip(step)

    def finish_sample(q):
        sb_copy(q, 0).wait_recv()
        each_chip(lambda d: sb_copy(q, d).wait_recv())
        hi, lo = split2(ypanel[q])
        y2[q, :, 0:B] = hi
        y2[q, :, B : 2 * B] = lo
        yhi[:, lanes(q)] = hi
        ylo[:, lanes(q)] = lo

    def gram_rows(q):
        dims = (((0,), (0,)), ((), ()))
        upto = slice(0, (q + 1) * B)
        hi_q, lo_q = yhi[:, lanes(q)], ylo[:, lanes(q)]
        g = lax.dot_general(hi_q, yhi[:, upto], dims, preferred_element_type=F32)
        g += lax.dot_general(hi_q, ylo[:, upto], dims, preferred_element_type=F32)
        g += lax.dot_general(lo_q, yhi[:, upto], dims, preferred_element_type=F32)
        g = g * (1.0 / (RB_DEV * B))
        g_out[0, lanes(q), upto] = g
        for j in range(q):
            g_out[0, lanes(j), lanes(q)] = g[:, lanes(j)].T

    def piece(i):
        return slice(i * PIECE, (i + 1) * PIECE)

    def inward(q, i, center):
        dst = zcross if center else zin
        sem = zx_r if center else zc_r
        return remote(
            zpart.at[q, piece(i), :], dst.at[q, piece(i), :], zc_s.at[q, i], sem.at[q, i], (inner, c)
        )

    def outward(q, i):
        part = z_out.at[piece(i), lanes(q)]
        return remote(part, part, zt_s.at[q, i], zt_r.at[q, i], (outer, c))

    def onward(q, i):
        part = z_out.at[piece(i), lanes(q)]
        return remote(part, part, zf_s.at[q, i], zt_r.at[q, i], (outer, c))

    def finish_piece(q, i):
        @pl.when(is_center)
        def _():
            inward(q, i, True).wait_recv()
            z_out[piece(i), lanes(q)] = zpart[q, piece(i), :] + zcross[q, piece(i), :]

            @pl.when(has_outer)
            def _():
                outward(q, i).start()

    def chain_piece(q, i):
        if i % (B // PIECE) == 0:
            rows = lanes(i * PIECE // B)
            both = jnp.dot(a_t[rows, :], y2[q], preferred_element_type=F32)
            zpart[q, rows, :] = both[:, :B] + both[:, B:]

        @pl.when(has_outer)
        def _():
            inward(q, i, False).wait_recv()
            zpart[q, piece(i), :] += zin[q, piece(i), :]

        @pl.when(is_center)
        def _():
            inward(q, i, True).start()

        @pl.when(not_center)
        def _():
            inward(q, i, False).start()

    place(codes, tiles_f, a_mat, 0, a_rows, CB_DEV, row_code)
    for cp in init:
        cp.wait_recv()
    place(sib_codes, sib_tiles, a_mat, ctx, a_rows, CB_DEV, row_code)
    partial_sample(0)
    send_sample(0)
    partial_sample(1)
    send_sample(1)
    for s in range(slots):
        tile_t[s] = tiles_f[s].T
    place(codes, tile_t, a_t, 0, CB_DEV, RB_DEV, lambda i, j: j * CB_DEV + i)
    reduce_sample(0)
    partial_sample(2)
    send_sample(2)
    reduce_sample(1)
    swap_sample(0)
    partial_sample(3)
    send_sample(3)
    finish_sample(0)

    between = {
        (0, 1): lambda: reduce_sample(2),
        (0, 3): lambda: swap_sample(1),
        (0, 5): lambda: reduce_sample(3),
        (0, 7): lambda: finish_sample(1),
        (1, 1): lambda: gram_rows(0),
        (1, 2): lambda: swap_sample(2),
        (1, 4): lambda: gram_rows(1),
        (1, 7): lambda: finish_sample(2),
        (2, 1): lambda: swap_sample(3),
        (2, 3): lambda: gram_rows(2),
        (2, 7): lambda: finish_sample(3),
        (3, 3): lambda: gram_rows(3),
    }
    late = []
    for q in range(chunks):
        for i in range(pieces):
            chain_piece(q, i)
            late.append((q, i))
            if len(late) > LAG:
                finish_piece(*late.pop(0))
            if (q, i) in between:
                between[q, i]()
    for item in late:
        finish_piece(*item)

    for q in range(chunks):
        for i in range(pieces):

            @pl.when(not_center)
            def _():
                outward(q, i).wait_recv()

            if n_rows > 4:

                @pl.when(jnp.logical_and(has_outer, not_center))
                def _():
                    onward(q, i).start()

    for cp in (*init, *om_swap):
        cp.wait_send()
    for q in range(chunks):
        each_chip(lambda d: rs_copy(q, d).wait_send())
        each_chip(lambda d: ag_copy(q, d).wait_send())
        sb_copy(q, 0).wait_send()
        each_chip(lambda d: sb_copy(q, d).wait_send())
        for i in range(pieces):
            inward(q, i, True).wait_send()

            @pl.when(jnp.logical_and(is_center, has_outer))
            def _():
                outward(q, i).wait_send()

            if n_rows > 4:

                @pl.when(jnp.logical_and(has_outer, not_center))
                def _():
                    onward(q, i).wait_send()


def solution(mesh):
    n_rows, n_cols = mesh.shape["rows"], mesh.shape["cols"]

    def local(tile_values, tile_rows, tile_cols, live_counts, test_block):
        slots = tile_values.shape[2]
        test_cols = test_block.shape[1]
        m = n_cols // 2
        panel, ctx = RB_DEV * B, CB_DEV * B
        chunks = test_cols // B
        pieces = ctx // PIECE
        share = panel // n_cols
        used = m * B if share == B else panel
        vmem = pl.BlockSpec(memory_space=pltpu.VMEM)
        smem = pl.BlockSpec(memory_space=pltpu.SMEM)
        hbm = pl.BlockSpec(memory_space=pltpu.HBM)
        dma = pltpu.SemaphoreType.DMA
        return pl.pallas_call(
            functools.partial(kernel, n_rows, n_cols, slots),
            out_shape=(
                jax.ShapeDtypeStruct((panel // n_cols, test_cols), F32),
                jax.ShapeDtypeStruct((ctx, test_cols), F32),
                jax.ShapeDtypeStruct((1, test_cols, test_cols), F32),
            ),
            in_specs=[smem, smem, smem, hbm, hbm],
            out_specs=(vmem, vmem, vmem),
            scratch_shapes=[
                pltpu.VMEM((slots, 8, B), jnp.int32),
                pltpu.VMEM((slots, 8, B), jnp.int32),
                pltpu.VMEM((slots, B, B), BF16),
                pltpu.VMEM((slots, B, B), F32),
                pltpu.VMEM((slots, B, B), F32),
                pltpu.VMEM((slots, B, B), F32),
                pltpu.VMEM((chunks, ctx, B), F32),
                pltpu.VMEM((chunks, ctx, B), F32),
                pltpu.VMEM((chunks, 2 * ctx, 2 * B), BF16),
                pltpu.VMEM((used, 2 * ctx), BF16),
                pltpu.VMEM((ctx, panel), BF16),
                pltpu.VMEM((chunks, used, B), F32),
                pltpu.VMEM((chunks, m - 1, share, B), F32),
                pltpu.VMEM((chunks, panel, B), F32),
                pltpu.VMEM((chunks, panel, 2 * B), BF16),
                pltpu.VMEM((panel, test_cols), BF16),
                pltpu.VMEM((panel, test_cols), BF16),
                pltpu.VMEM((chunks, ctx, B), F32),
                pltpu.VMEM((chunks, ctx, B), F32),
                pltpu.VMEM((chunks, ctx, B), F32),
                dma((1 + chunks,)),
                dma((2,)), dma((2,)),
                dma((chunks,)), dma((chunks,)),
                dma((chunks, m - 1)), dma((chunks, m - 1)),
                dma((chunks, m - 1)), dma((chunks, m - 1)),
                dma((chunks, m)), dma((chunks, m)),
                dma((chunks, pieces)), dma((chunks, pieces)), dma((chunks, pieces)),
                dma((chunks, pieces)), dma((chunks, pieces)), dma((chunks, pieces)),
            ],
            compiler_params=pltpu.CompilerParams(
                collective_id=0, has_side_effects=True, vmem_limit_bytes=60 * 1024 * 1024
            ),
            cost_estimate=pl.CostEstimate(flops=4_000_000_000, bytes_accessed=4_000_000, transcendentals=0),
        )(tile_rows, tile_cols, live_counts, tile_values, test_block)

    return jax.shard_map(
        local,
        mesh=mesh,
        in_specs=(
            P("rows", "cols", None, None, None),
            P("rows", "cols", None),
            P("rows", "cols", None),
            P("rows", "cols"),
            P("cols", None),
        ),
        out_specs=(P(("rows", "cols"), None), P("cols", None), P("rows", None, None)),
        check_vma=False,
    )
```

```python
import functools

import jax
import jax.numpy as jnp
from jax import lax
from jax.experimental import pallas as pl
from jax.experimental.pallas import tpu as pltpu
from jax.sharding import PartitionSpec as P

RB_DEV = 8
CB_DEV = 4
B = 128
MESH = pl.DeviceIdType.MESH
F32 = jnp.float32
BF16 = jnp.bfloat16
LAG = 5
PIECE = 64


def split2(x):
    hi = x.astype(BF16)
    return hi, (x - hi.astype(F32)).astype(BF16)


def kernel(
    n_rows, n_cols, slots,
    rows_ref, cols_ref, live_ref, tiles_ref, om_ref,
    y_out, z_out, g_out,
    codes, tiles_in, tiles_f, tile_t, om_in, om2, a_mat, a_t,
    ypart, xrecv, rs_recv, ypanel, y2, yhi, ylo, zpart, zin, zcross,
    load_s, xs_s, xs_r, rs_s, rs_r, ag_s, ag_r, sb_s, sb_r,
    zc_s, zc_r, zx_r, zt_s, zt_r, zf_s,
):
    r = lax.axis_index("rows")
    c = lax.axis_index("cols")
    core = lax.rem(c, 2)
    chip = c // 2
    other = 1 - core
    sib = chip * 2 + other
    m = n_cols // 2
    panel = RB_DEV * B
    ctx = CB_DEV * B
    share = panel // n_cols
    compact = share == B
    chunks = om_ref.shape[1] // B
    pieces = ctx // PIECE
    mid = n_rows // 2
    lower = r < mid
    inner = jnp.where(lower, r + 1, r - 1)
    outer = jnp.where(lower, r - 1, r + 1)
    is_center = jnp.logical_or(r == mid - 1, r == mid)
    not_center = jnp.logical_not(is_center)
    has_outer = jnp.logical_and(r > 0, r < n_rows - 1)

    def remote(src, dst, ssem, rsem, dev):
        return pltpu.make_async_remote_copy(
            src_ref=src, dst_ref=dst, send_sem=ssem, recv_sem=rsem, device_id=dev, device_id_type=MESH
        )

    def each_chip(fn):
        def body(d, _):
            fn(d)
            return 0

        lax.fori_loop(1, m, body, 0)

    def lanes(q):
        return slice(q * B, (q + 1) * B)

    load_tiles = pltpu.make_async_copy(tiles_ref.at[0, 0], tiles_in, load_s.at[0])
    load_om = [
        pltpu.make_async_copy(om_ref.at[:, lanes(q)], om_in.at[q], load_s.at[1 + q]) for q in range(chunks)
    ]
    load_tiles.start()
    for cp in load_om:
        cp.start()

    barrier = pltpu.get_barrier_semaphore()
    pl.semaphore_signal(barrier, inc=1, device_id=(r, sib), device_id_type=MESH)

    def greet_chip(d):
        pl.semaphore_signal(
            barrier, inc=1, device_id=(r, lax.rem(chip + d, m) * 2 + core), device_id_type=MESH
        )

    each_chip(greet_chip)

    def greet_row(d, _):
        pl.semaphore_signal(barrier, inc=1, device_id=(lax.rem(r + d, n_rows), c), device_id_type=MESH)
        return 0

    lax.fori_loop(1, n_rows, greet_row, 0)

    load_tiles.wait()
    for s in range(slots):
        code = jnp.where(
            s < live_ref[0, 0], rows_ref[0, 0, s] * CB_DEV + cols_ref[0, 0, s], -1
        )
        codes[s] = jnp.full((8, B), code, jnp.int32)
        tiles_f[s] = tiles_in[s].astype(F32)

    def place(code_ref, source, target, col0, rows, cols, want):
        def line(i, _):
            for j in range(cols):
                code = want(i, j)
                val = jnp.zeros((B // 8, 8, B), F32)
                for s in range(slots):
                    hit = jnp.broadcast_to((code_ref[s] == code)[None], val.shape)
                    val = jnp.where(hit, source[s].reshape(val.shape), val)
                target[pl.ds(pl.multiple_of(i * B, B), B), col0 + j * B : col0 + (j + 1) * B] = (
                    val.reshape(B, B).astype(BF16)
                )
            return 0

        lax.fori_loop(0, rows, line, 0)

    if compact:

        def row_code(i, j):
            parity = jnp.where(i < m, other, core)
            return (2 * lax.rem(i, m) + parity) * CB_DEV + j

    else:

        def row_code(i, j):
            return i * CB_DEV + j

    def part_rows(j, mine):
        if compact:
            start = (j + (m if mine else 0)) * share
        else:
            start = (2 * j + (core if mine else other)) * share
        return pl.ds(pl.multiple_of(start, 8), share)

    def panel_rows(j, parity):
        return pl.ds(pl.multiple_of((2 * j + parity) * share, 8), share)

    def rs_copy(q, d):
        j = lax.rem(chip + d, m)
        return remote(
            ypart.at[q, part_rows(j, True), :], rs_recv.at[q, d - 1], rs_s.at[q, d - 1], rs_r.at[q, d - 1],
            (r, j * 2 + core),
        )

    def ag_copy(q, d):
        j = lax.rem(chip + d, m)
        mine = ypanel.at[q, panel_rows(chip, core), :]
        return remote(mine, mine, ag_s.at[q, d - 1], ag_r.at[q, d - 1], (r, j * 2 + core))

    def sb_copy(q, d):
        block = ypanel.at[q, panel_rows(lax.rem(chip + m - d, m), core), :]
        return remote(block, block, sb_s.at[q, d], sb_r.at[q, d], (r, sib))

    def xs_copy(q, d):
        j = lax.rem(chip + d, m)
        return remote(
            ypart.at[q, part_rows(j, False), :], xrecv.at[q, d], xs_s.at[q, d], xs_r.at[q, d], (r, sib)
        )

    def partial_sample(q):
        load_om[q].wait()
        hi, lo = split2(om_in[q])
        om2[q, :, 0:B] = hi
        om2[q, :, B : 2 * B] = lo
        step = 2 * B
        for k in range(panel // step):
            rows = slice(k * step, (k + 1) * step)
            both = jnp.dot(a_mat[rows, :], om2[q], preferred_element_type=F32)
            ypart[q, rows, :] = both[:, :B] + both[:, B:]

    def swap_partial(q):
        each_chip(lambda d: xs_copy(q, d).start())
        xs_copy(q, 0).start()

    def send_sample(q):
        def step(d):
            xs_copy(q, d).wait_recv()
            ypart[q, part_rows(lax.rem(chip + d, m), True), :] += xrecv[q, d]
            rs_copy(q, d).start()

        each_chip(step)

    def reduce_sample(q):
        xs_copy(q, 0).wait_recv()
        total = ypart[q, part_rows(chip, True), :] + xrecv[q, 0]
        each_chip(lambda d: rs_copy(q, d).wait_recv())
        for d in range(m - 1):
            total = total + rs_recv[q, d]
        ypanel[q, panel_rows(chip, core), :] = total
        each_chip(lambda d: ag_copy(q, d).start())
        sb_copy(q, 0).start()
        y_out[:, lanes(q)] = total

    def swap_sample(q):
        def step(d):
            ag_copy(q, d).wait_recv()
            sb_copy(q, d).start()

        each_chip(step)

    def finish_sample(q):
        sb_copy(q, 0).wait_recv()
        each_chip(lambda d: sb_copy(q, d).wait_recv())
        hi, lo = split2(ypanel[q])
        y2[q, :, 0:B] = hi
        y2[q, :, B : 2 * B] = lo
        yhi[:, lanes(q)] = hi
        ylo[:, lanes(q)] = lo

    def gram_rows(q):
        dims = (((0,), (0,)), ((), ()))
        upto = slice(0, (q + 1) * B)
        hi_q, lo_q = yhi[:, lanes(q)], ylo[:, lanes(q)]
        g = lax.dot_general(hi_q, yhi[:, upto], dims, preferred_element_type=F32)
        g += lax.dot_general(hi_q, ylo[:, upto], dims, preferred_element_type=F32)
        g += lax.dot_general(lo_q, yhi[:, upto], dims, preferred_element_type=F32)
        g = g * (1.0 / (RB_DEV * B))
        g_out[0, lanes(q), upto] = g
        for j in range(q):
            g_out[0, lanes(j), lanes(q)] = g[:, lanes(j)].T

    def piece(i):
        return slice(i * PIECE, (i + 1) * PIECE)

    def inward(q, i, center):
        dst = zcross if center else zin
        sem = zx_r if center else zc_r
        return remote(
            zpart.at[q, piece(i), :], dst.at[q, piece(i), :], zc_s.at[q, i], sem.at[q, i], (inner, c)
        )

    def outward(q, i):
        part = z_out.at[piece(i), lanes(q)]
        return remote(part, part, zt_s.at[q, i], zt_r.at[q, i], (outer, c))

    def onward(q, i):
        part = z_out.at[piece(i), lanes(q)]
        return remote(part, part, zf_s.at[q, i], zt_r.at[q, i], (outer, c))

    def finish_piece(q, i):
        @pl.when(is_center)
        def _():
            inward(q, i, True).wait_recv()
            z_out[piece(i), lanes(q)] = zpart[q, piece(i), :] + zcross[q, piece(i), :]

            @pl.when(has_outer)
            def _():
                outward(q, i).start()

    def chain_piece(q, i):
        if i % (B // PIECE) == 0:
            rows = lanes(i * PIECE // B)
            both = jnp.dot(a_t[rows, :], y2[q], preferred_element_type=F32)
            zpart[q, rows, :] = both[:, :B] + both[:, B:]

        @pl.when(has_outer)
        def _():
            inward(q, i, False).wait_recv()
            zpart[q, piece(i), :] += zin[q, piece(i), :]

        @pl.when(is_center)
        def _():
            inward(q, i, True).start()

        @pl.when(not_center)
        def _():
            inward(q, i, False).start()

    place(codes, tiles_f, a_mat, 0, RB_DEV, CB_DEV, row_code)
    partial_sample(0)
    pl.semaphore_wait(barrier, 1 + (m - 1) + (n_rows - 1))
    swap_partial(0)
    partial_sample(1)
    swap_partial(1)
    send_sample(0)
    for s in range(slots):
        tile_t[s] = tiles_f[s].T
    place(codes, tile_t, a_t, 0, CB_DEV, RB_DEV, lambda i, j: j * CB_DEV + i)
    send_sample(1)
    reduce_sample(0)
    partial_sample(2)
    swap_partial(2)
    reduce_sample(1)
    send_sample(2)
    swap_sample(0)
    partial_sample(3)
    swap_partial(3)
    finish_sample(0)

    between = {
        (0, 0): lambda: send_sample(3),
        (0, 1): lambda: reduce_sample(2),
        (0, 3): lambda: swap_sample(1),
        (0, 5): lambda: reduce_sample(3),
        (0, 7): lambda: finish_sample(1),
        (1, 1): lambda: gram_rows(0),
        (1, 2): lambda: swap_sample(2),
        (1, 4): lambda: gram_rows(1),
        (1, 7): lambda: finish_sample(2),
        (2, 1): lambda: swap_sample(3),
        (2, 3): lambda: gram_rows(2),
        (2, 7): lambda: finish_sample(3),
        (3, 3): lambda: gram_rows(3),
    }
    late = []
    for q in range(chunks):
        for i in range(pieces):
            chain_piece(q, i)
            late.append((q, i))
            if len(late) > LAG:
                finish_piece(*late.pop(0))
            if (q, i) in between:
                between[q, i]()
    for item in late:
        finish_piece(*item)

    for q in range(chunks):
        for i in range(pieces):

            @pl.when(not_center)
            def _():
                outward(q, i).wait_recv()

            if n_rows > 4:

                @pl.when(jnp.logical_and(has_outer, not_center))
                def _():
                    onward(q, i).start()

    for q in range(chunks):
        xs_copy(q, 0).wait_send()
        each_chip(lambda d: xs_copy(q, d).wait_send())
        each_chip(lambda d: rs_copy(q, d).wait_send())
        each_chip(lambda d: ag_copy(q, d).wait_send())
        sb_copy(q, 0).wait_send()
        each_chip(lambda d: sb_copy(q, d).wait_send())
        for i in range(pieces):
            inward(q, i, True).wait_send()

            @pl.when(jnp.logical_and(is_center, has_outer))
            def _():
                outward(q, i).wait_send()

            if n_rows > 4:

                @pl.when(jnp.logical_and(has_outer, not_center))
                def _():
                    onward(q, i).wait_send()


def solution(mesh):
    n_rows, n_cols = mesh.shape["rows"], mesh.shape["cols"]

    def local(tile_values, tile_rows, tile_cols, live_counts, test_block):
        slots = tile_values.shape[2]
        test_cols = test_block.shape[1]
        m = n_cols // 2
        panel, ctx = RB_DEV * B, CB_DEV * B
        chunks = test_cols // B
        pieces = ctx // PIECE
        share = panel // n_cols
        vmem = pl.BlockSpec(memory_space=pltpu.VMEM)
        smem = pl.BlockSpec(memory_space=pltpu.SMEM)
        hbm = pl.BlockSpec(memory_space=pltpu.HBM)
        dma = pltpu.SemaphoreType.DMA
        return pl.pallas_call(
            functools.partial(kernel, n_rows, n_cols, slots),
            out_shape=(
                jax.ShapeDtypeStruct((panel // n_cols, test_cols), F32),
                jax.ShapeDtypeStruct((ctx, test_cols), F32),
                jax.ShapeDtypeStruct((1, test_cols, test_cols), F32),
            ),
            in_specs=[smem, smem, smem, hbm, hbm],
            out_specs=(vmem, vmem, vmem),
            scratch_shapes=[
                pltpu.VMEM((slots, 8, B), jnp.int32),
                pltpu.VMEM((slots, B, B), BF16),
                pltpu.VMEM((slots, B, B), F32),
                pltpu.VMEM((slots, B, B), F32),
                pltpu.VMEM((chunks, ctx, B), F32),
                pltpu.VMEM((chunks, ctx, 2 * B), BF16),
                pltpu.VMEM((panel, ctx), BF16),
                pltpu.VMEM((ctx, panel), BF16),
                pltpu.VMEM((chunks, panel, B), F32),
                pltpu.VMEM((chunks, m, share, B), F32),
                pltpu.VMEM((chunks, m - 1, share, B), F32),
                pltpu.VMEM((chunks, panel, B), F32),
                pltpu.VMEM((chunks, panel, 2 * B), BF16),
                pltpu.VMEM((panel, test_cols), BF16),
                pltpu.VMEM((panel, test_cols), BF16),
                pltpu.VMEM((chunks, ctx, B), F32),
                pltpu.VMEM((chunks, ctx, B), F32),
                pltpu.VMEM((chunks, ctx, B), F32),
                dma((1 + chunks,)),
                dma((chunks, m)), dma((chunks, m)),
                dma((chunks, m - 1)), dma((chunks, m - 1)),
                dma((chunks, m - 1)), dma((chunks, m - 1)),
                dma((chunks, m)), dma((chunks, m)),
                dma((chunks, pieces)), dma((chunks, pieces)), dma((chunks, pieces)),
                dma((chunks, pieces)), dma((chunks, pieces)), dma((chunks, pieces)),
            ],
            compiler_params=pltpu.CompilerParams(
                collective_id=0, has_side_effects=True, vmem_limit_bytes=51 * 1024 * 1024
            ),
            cost_estimate=pl.CostEstimate(flops=4_000_000_000, bytes_accessed=4_000_000, transcendentals=0),
        )(tile_rows, tile_cols, live_counts, tile_values, test_block)

    return jax.shard_map(
        local,
        mesh=mesh,
        in_specs=(
            P("rows", "cols", None, None, None),
            P("rows", "cols", None),
            P("rows", "cols", None),
            P("rows", "cols"),
            P("cols", None),
        ),
        out_specs=(P(("rows", "cols"), None), P("cols", None), P("rows", None, None)),
        check_vma=False,
    )
```

```python
import functools

import jax
import jax.numpy as jnp
from jax import lax
from jax.experimental import pallas as pl
from jax.experimental.pallas import tpu as pltpu
from jax.sharding import PartitionSpec as P

RB_DEV = 8
CB_DEV = 4
B = 128
MESH = pl.DeviceIdType.MESH
F32 = jnp.float32
BF16 = jnp.bfloat16
LAG = 5
PIECE = 64


def split2(x):
    hi = x.astype(BF16)
    return hi, (x - hi.astype(F32)).astype(BF16)


def kernel(
    n_rows, n_cols, slots,
    rows_ref, cols_ref, live_ref, tiles_ref, om_ref,
    y_out, z_out, g_out,
    codes, tiles_in, tiles_f, tile_t, om_in, om2, a_mat, a_t,
    ypart, xrecv, rs_recv, ypanel, y2, zpart, zin, zcross,
    load_s, xs_s, xs_r, rs_s, rs_r, ag_s, ag_r, sb_s, sb_r,
    zc_s, zc_r, zx_r, zt_s, zt_r, zf_s,
):
    r = lax.axis_index("rows")
    c = lax.axis_index("cols")
    core = lax.rem(c, 2)
    chip = c // 2
    other = 1 - core
    sib = chip * 2 + other
    m = n_cols // 2
    panel = RB_DEV * B
    ctx = CB_DEV * B
    share = panel // n_cols
    compact = share == B
    chunks = om_ref.shape[1] // B
    pieces = ctx // PIECE
    mid = n_rows // 2
    lower = r < mid
    inner = jnp.where(lower, r + 1, r - 1)
    outer = jnp.where(lower, r - 1, r + 1)
    is_center = jnp.logical_or(r == mid - 1, r == mid)
    not_center = jnp.logical_not(is_center)
    has_outer = jnp.logical_and(r > 0, r < n_rows - 1)

    def remote(src, dst, ssem, rsem, dev):
        return pltpu.make_async_remote_copy(
            src_ref=src, dst_ref=dst, send_sem=ssem, recv_sem=rsem, device_id=dev, device_id_type=MESH
        )

    def each_chip(fn):
        def body(d, _):
            fn(d)
            return 0

        lax.fori_loop(1, m, body, 0)

    def lanes(q):
        return slice(q * B, (q + 1) * B)

    load_tiles = pltpu.make_async_copy(tiles_ref.at[0, 0], tiles_in, load_s.at[0])
    load_om = [
        pltpu.make_async_copy(om_ref.at[:, lanes(q)], om_in.at[q], load_s.at[1 + q]) for q in range(chunks)
    ]
    load_tiles.start()
    for cp in load_om:
        cp.start()

    barrier = pltpu.get_barrier_semaphore()
    pl.semaphore_signal(barrier, inc=1, device_id=(r, sib), device_id_type=MESH)

    def greet_chip(d):
        pl.semaphore_signal(
            barrier, inc=1, device_id=(r, lax.rem(chip + d, m) * 2 + core), device_id_type=MESH
        )

    each_chip(greet_chip)

    def greet_row(d, _):
        pl.semaphore_signal(barrier, inc=1, device_id=(lax.rem(r + d, n_rows), c), device_id_type=MESH)
        return 0

    lax.fori_loop(1, n_rows, greet_row, 0)

    load_tiles.wait()
    for s in range(slots):
        code = jnp.where(
            s < live_ref[0, 0], rows_ref[0, 0, s] * CB_DEV + cols_ref[0, 0, s], -1
        )
        codes[s] = jnp.full((8, B), code, jnp.int32)
        tiles_f[s] = tiles_in[s].astype(F32)

    def place(code_ref, source, target, col0, rows, cols, want):
        def line(i, _):
            for j in range(cols):
                code = want(i, j)
                val = jnp.zeros((B // 8, 8, B), F32)
                for s in range(slots):
                    hit = jnp.broadcast_to((code_ref[s] == code)[None], val.shape)
                    val = jnp.where(hit, source[s].reshape(val.shape), val)
                target[pl.ds(pl.multiple_of(i * B, B), B), col0 + j * B : col0 + (j + 1) * B] = (
                    val.reshape(B, B).astype(BF16)
                )
            return 0

        lax.fori_loop(0, rows, line, 0)

    if compact:

        def row_code(i, j):
            parity = jnp.where(i < m, other, core)
            return (2 * lax.rem(i, m) + parity) * CB_DEV + j

    else:

        def row_code(i, j):
            return i * CB_DEV + j

    def part_rows(j, mine):
        if compact:
            start = (j + (m if mine else 0)) * share
        else:
            start = (2 * j + (core if mine else other)) * share
        return pl.ds(pl.multiple_of(start, 8), share)

    def panel_rows(j, parity):
        return pl.ds(pl.multiple_of((2 * j + parity) * share, 8), share)

    def rs_copy(q, d):
        j = lax.rem(chip + d, m)
        return remote(
            ypart.at[q, part_rows(j, True), :], rs_recv.at[q, d - 1], rs_s.at[q, d - 1], rs_r.at[q, d - 1],
            (r, j * 2 + core),
        )

    def ag_copy(q, d):
        j = lax.rem(chip + d, m)
        mine = ypanel.at[q, panel_rows(chip, core), :]
        return remote(mine, mine, ag_s.at[q, d - 1], ag_r.at[q, d - 1], (r, j * 2 + core))

    def sb_copy(q, d):
        block = ypanel.at[q, panel_rows(lax.rem(chip + m - d, m), core), :]
        return remote(block, block, sb_s.at[q, d], sb_r.at[q, d], (r, sib))

    def xs_copy(q, d):
        j = lax.rem(chip + d, m)
        return remote(
            ypart.at[q, part_rows(j, False), :], xrecv.at[q, d], xs_s.at[q, d], xs_r.at[q, d], (r, sib)
        )

    def partial_sample(q):
        load_om[q].wait()
        hi, lo = split2(om_in[q])
        om2[q, :, 0:B] = hi
        om2[q, :, B : 2 * B] = lo
        step = 2 * B
        for k in range(panel // step):
            rows = slice(k * step, (k + 1) * step)
            both = jnp.dot(a_mat[rows, :], om2[q], preferred_element_type=F32)
            ypart[q, rows, :] = both[:, :B] + both[:, B:]

    def swap_partial(q):
        each_chip(lambda d: xs_copy(q, d).start())
        xs_copy(q, 0).start()

    def send_sample(q):
        def step(d):
            xs_copy(q, d).wait_recv()
            ypart[q, part_rows(lax.rem(chip + d, m), True), :] += xrecv[q, d]
            rs_copy(q, d).start()

        each_chip(step)

    def reduce_sample(q):
        xs_copy(q, 0).wait_recv()
        total = ypart[q, part_rows(chip, True), :] + xrecv[q, 0]
        each_chip(lambda d: rs_copy(q, d).wait_recv())
        for d in range(m - 1):
            total = total + rs_recv[q, d]
        ypanel[q, panel_rows(chip, core), :] = total
        each_chip(lambda d: ag_copy(q, d).start())
        sb_copy(q, 0).start()
        y_out[:, lanes(q)] = total

    def swap_sample(q):
        def step(d):
            ag_copy(q, d).wait_recv()
            sb_copy(q, d).start()

        each_chip(step)

    def finish_sample(q):
        sb_copy(q, 0).wait_recv()
        each_chip(lambda d: sb_copy(q, d).wait_recv())
        hi, lo = split2(ypanel[q])
        y2[:, 2 * q * B : (2 * q + 1) * B] = hi
        y2[:, (2 * q + 1) * B : (2 * q + 2) * B] = lo

    def gram_rows(q):
        dims = (((0,), (0,)), ((), ()))
        own = slice(2 * q * B, (2 * q + 2) * B)
        parts = lax.dot_general(y2[:, own], y2[:, : own.stop], dims, preferred_element_type=F32)
        both = parts[:B, :] + parts[B:, :]
        for j in range(q + 1):
            g = both[:, 2 * j * B : (2 * j + 1) * B] + both[:, (2 * j + 1) * B : (2 * j + 2) * B]
            g = g * (1.0 / (RB_DEV * B))
            g_out[0, lanes(q), lanes(j)] = g
            if j < q:
                g_out[0, lanes(j), lanes(q)] = g.T

    def piece(i):
        return slice(i * PIECE, (i + 1) * PIECE)

    def inward(q, i, center):
        dst = zcross if center else zin
        sem = zx_r if center else zc_r
        return remote(
            zpart.at[q, piece(i), :], dst.at[q, piece(i), :], zc_s.at[q, i], sem.at[q, i], (inner, c)
        )

    def outward(q, i):
        part = z_out.at[piece(i), lanes(q)]
        return remote(part, part, zt_s.at[q, i], zt_r.at[q, i], (outer, c))

    def onward(q, i):
        part = z_out.at[piece(i), lanes(q)]
        return remote(part, part, zf_s.at[q, i], zt_r.at[q, i], (outer, c))

    def finish_piece(q, i):
        @pl.when(is_center)
        def _():
            inward(q, i, True).wait_recv()
            z_out[piece(i), lanes(q)] = zpart[q, piece(i), :] + zcross[q, piece(i), :]

            @pl.when(has_outer)
            def _():
                outward(q, i).start()

    def chain_piece(q, i):
        if i % (B // PIECE) == 0:
            rows = lanes(i * PIECE // B)
            both = jnp.dot(a_t[rows, :], y2[:, 2 * q * B : (2 * q + 2) * B], preferred_element_type=F32)
            zpart[q, rows, :] = both[:, :B] + both[:, B:]

        @pl.when(has_outer)
        def _():
            inward(q, i, False).wait_recv()
            zpart[q, piece(i), :] += zin[q, piece(i), :]

        @pl.when(is_center)
        def _():
            inward(q, i, True).start()

        @pl.when(not_center)
        def _():
            inward(q, i, False).start()

    place(codes, tiles_f, a_mat, 0, RB_DEV, CB_DEV, row_code)
    partial_sample(0)
    pl.semaphore_wait(barrier, 1 + (m - 1) + (n_rows - 1))
    swap_partial(0)
    partial_sample(1)
    swap_partial(1)
    send_sample(0)
    for s in range(slots):
        tile_t[s] = tiles_f[s].T
    place(codes, tile_t, a_t, 0, CB_DEV, RB_DEV, lambda i, j: j * CB_DEV + i)
    send_sample(1)
    reduce_sample(0)
    partial_sample(2)
    swap_partial(2)
    reduce_sample(1)
    send_sample(2)
    swap_sample(0)
    partial_sample(3)
    swap_partial(3)
    finish_sample(0)

    between = {
        (0, 0): lambda: send_sample(3),
        (0, 1): lambda: reduce_sample(2),
        (0, 3): lambda: swap_sample(1),
        (0, 5): lambda: reduce_sample(3),
        (0, 7): lambda: finish_sample(1),
        (1, 2): lambda: swap_sample(2),
        (1, 7): lambda: finish_sample(2),
        (2, 1): lambda: swap_sample(3),
        (2, 7): lambda: finish_sample(3),
    }
    late = []
    for q in range(chunks):
        for i in range(pieces):
            chain_piece(q, i)
            late.append((q, i))
            if len(late) > LAG:
                finish_piece(*late.pop(0))
            if (q, i) in between:
                between[q, i]()
    for item in late:
        finish_piece(*item)
    for q in range(chunks):
        gram_rows(q)

    for q in range(chunks):
        for i in range(pieces):

            @pl.when(not_center)
            def _():
                outward(q, i).wait_recv()

            if n_rows > 4:

                @pl.when(jnp.logical_and(has_outer, not_center))
                def _():
                    onward(q, i).start()

    for q in range(chunks):
        xs_copy(q, 0).wait_send()
        each_chip(lambda d: xs_copy(q, d).wait_send())
        each_chip(lambda d: rs_copy(q, d).wait_send())
        each_chip(lambda d: ag_copy(q, d).wait_send())
        sb_copy(q, 0).wait_send()
        each_chip(lambda d: sb_copy(q, d).wait_send())
        for i in range(pieces):
            inward(q, i, True).wait_send()

            @pl.when(jnp.logical_and(is_center, has_outer))
            def _():
                outward(q, i).wait_send()

            if n_rows > 4:

                @pl.when(jnp.logical_and(has_outer, not_center))
                def _():
                    onward(q, i).wait_send()


def solution(mesh):
    n_rows, n_cols = mesh.shape["rows"], mesh.shape["cols"]

    def local(tile_values, tile_rows, tile_cols, live_counts, test_block):
        slots = tile_values.shape[2]
        test_cols = test_block.shape[1]
        m = n_cols // 2
        panel, ctx = RB_DEV * B, CB_DEV * B
        chunks = test_cols // B
        pieces = ctx // PIECE
        share = panel // n_cols
        vmem = pl.BlockSpec(memory_space=pltpu.VMEM)
        smem = pl.BlockSpec(memory_space=pltpu.SMEM)
        hbm = pl.BlockSpec(memory_space=pltpu.HBM)
        dma = pltpu.SemaphoreType.DMA
        return pl.pallas_call(
            functools.partial(kernel, n_rows, n_cols, slots),
            out_shape=(
                jax.ShapeDtypeStruct((panel // n_cols, test_cols), F32),
                jax.ShapeDtypeStruct((ctx, test_cols), F32),
                jax.ShapeDtypeStruct((1, test_cols, test_cols), F32),
            ),
            in_specs=[smem, smem, smem, hbm, hbm],
            out_specs=(vmem, vmem, vmem),
            scratch_shapes=[
                pltpu.VMEM((slots, 8, B), jnp.int32),
                pltpu.VMEM((slots, B, B), BF16),
                pltpu.VMEM((slots, B, B), F32),
                pltpu.VMEM((slots, B, B), F32),
                pltpu.VMEM((chunks, ctx, B), F32),
                pltpu.VMEM((chunks, ctx, 2 * B), BF16),
                pltpu.VMEM((panel, ctx), BF16),
                pltpu.VMEM((ctx, panel), BF16),
                pltpu.VMEM((chunks, panel, B), F32),
                pltpu.VMEM((chunks, m, share, B), F32),
                pltpu.VMEM((chunks, m - 1, share, B), F32),
                pltpu.VMEM((chunks, panel, B), F32),
                pltpu.VMEM((panel, 2 * test_cols), BF16),
                pltpu.VMEM((chunks, ctx, B), F32),
                pltpu.VMEM((chunks, ctx, B), F32),
                pltpu.VMEM((chunks, ctx, B), F32),
                dma((1 + chunks,)),
                dma((chunks, m)), dma((chunks, m)),
                dma((chunks, m - 1)), dma((chunks, m - 1)),
                dma((chunks, m - 1)), dma((chunks, m - 1)),
                dma((chunks, m)), dma((chunks, m)),
                dma((chunks, pieces)), dma((chunks, pieces)), dma((chunks, pieces)),
                dma((chunks, pieces)), dma((chunks, pieces)), dma((chunks, pieces)),
            ],
            compiler_params=pltpu.CompilerParams(
                collective_id=0, has_side_effects=True, vmem_limit_bytes=51 * 1024 * 1024
            ),
            cost_estimate=pl.CostEstimate(flops=4_000_000_000, bytes_accessed=4_000_000, transcendentals=0),
        )(tile_rows, tile_cols, live_counts, tile_values, test_block)

    return jax.shard_map(
        local,
        mesh=mesh,
        in_specs=(
            P("rows", "cols", None, None, None),
            P("rows", "cols", None),
            P("rows", "cols", None),
            P("rows", "cols"),
            P("cols", None),
        ),
        out_specs=(P(("rows", "cols"), None), P("cols", None), P("rows", None, None)),
        check_vma=False,
    )
```

```python
import functools

import jax
import jax.numpy as jnp
from jax import lax
from jax.experimental import pallas as pl
from jax.experimental.pallas import tpu as pltpu
from jax.sharding import PartitionSpec as P

RB_DEV = 8
CB_DEV = 4
B = 128
MESH = pl.DeviceIdType.MESH
F32 = jnp.float32
BF16 = jnp.bfloat16
LAG = 5
PIECE = 64


def split2(x):
    hi = x.astype(BF16)
    return hi, (x - hi.astype(F32)).astype(BF16)


def kernel(
    n_rows, n_cols, slots,
    rows_ref, cols_ref, live_ref, tiles_ref, om_ref,
    y_out, z_out, g_out,
    codes, tiles_in, tiles_f, tile_t, om_in, om2, a_mat, a_t,
    ypart, xrecv, rs_recv, ypanel, y2, zpart, zin, zcross,
    load_s, xs_s, xs_r, rs_s, rs_r, ag_s, ag_r, sb_s, sb_r,
    zc_s, zc_r, zx_r, zt_s, zt_r, zf_s,
):
    r = lax.axis_index("rows")
    c = lax.axis_index("cols")
    core = lax.rem(c, 2)
    chip = c // 2
    other = 1 - core
    sib = chip * 2 + other
    m = n_cols // 2
    panel = RB_DEV * B
    ctx = CB_DEV * B
    share = panel // n_cols
    compact = share == B
    chunks = om_ref.shape[1] // B
    pieces = ctx // PIECE
    mid = n_rows // 2
    lower = r < mid
    inner = jnp.where(lower, r + 1, r - 1)
    outer = jnp.where(lower, r - 1, r + 1)
    is_center = jnp.logical_or(r == mid - 1, r == mid)
    not_center = jnp.logical_not(is_center)
    has_outer = jnp.logical_and(r > 0, r < n_rows - 1)

    def remote(src, dst, ssem, rsem, dev):
        return pltpu.make_async_remote_copy(
            src_ref=src, dst_ref=dst, send_sem=ssem, recv_sem=rsem, device_id=dev, device_id_type=MESH
        )

    def each_chip(fn):
        def body(d, _):
            fn(d)
            return 0

        lax.fori_loop(1, m, body, 0)

    def lanes(q):
        return slice(q * B, (q + 1) * B)

    load_tiles = pltpu.make_async_copy(tiles_ref.at[0, 0], tiles_in, load_s.at[0])
    load_om = [
        pltpu.make_async_copy(om_ref.at[:, lanes(q)], om_in.at[q], load_s.at[1 + q]) for q in range(chunks)
    ]
    load_tiles.start()
    for cp in load_om:
        cp.start()

    barrier = pltpu.get_barrier_semaphore()
    pl.semaphore_signal(barrier, inc=1, device_id=(r, sib), device_id_type=MESH)

    def greet_chip(d):
        pl.semaphore_signal(
            barrier, inc=1, device_id=(r, lax.rem(chip + d, m) * 2 + core), device_id_type=MESH
        )

    each_chip(greet_chip)

    def greet_row(d, _):
        pl.semaphore_signal(barrier, inc=1, device_id=(lax.rem(r + d, n_rows), c), device_id_type=MESH)
        return 0

    lax.fori_loop(1, n_rows, greet_row, 0)

    load_tiles.wait()
    for s in range(slots):
        code = jnp.where(
            s < live_ref[0, 0], rows_ref[0, 0, s] * CB_DEV + cols_ref[0, 0, s], -1
        )
        codes[s] = jnp.full((8, B), code, jnp.int32)
        tiles_f[s] = tiles_in[s].astype(F32)

    def place(code_ref, source, target, first, end, cols, want):
        def line(i, _):
            for j in range(cols):
                code = want(i, j)
                val = jnp.zeros((B // 8, 8, B), F32)
                for s in range(slots):
                    hit = jnp.broadcast_to((code_ref[s] == code)[None], val.shape)
                    val = jnp.where(hit, source[s].reshape(val.shape), val)
                target[pl.ds(pl.multiple_of(i * B, B), B), j * B : (j + 1) * B] = (
                    val.reshape(B, B).astype(BF16)
                )
            return 0

        lax.fori_loop(first, end, line, 0)

    if compact:

        def row_code(i, j):
            parity = jnp.where(i < m, other, core)
            return (2 * lax.rem(i, m) + parity) * CB_DEV + j

    else:

        def row_code(i, j):
            return i * CB_DEV + j

    def part_rows(j, mine):
        if compact:
            start = (j + (m if mine else 0)) * share
        else:
            start = (2 * j + (core if mine else other)) * share
        return pl.ds(pl.multiple_of(start, 8), share)

    def panel_rows(j, parity):
        return pl.ds(pl.multiple_of((2 * j + parity) * share, 8), share)

    def rs_copy(q, d):
        j = lax.rem(chip + d, m)
        return remote(
            ypart.at[q, part_rows(j, True), :], rs_recv.at[q, d - 1], rs_s.at[q, d - 1], rs_r.at[q, d - 1],
            (r, j * 2 + core),
        )

    def ag_copy(q, d):
        j = lax.rem(chip + d, m)
        mine = ypanel.at[q, panel_rows(chip, core), :]
        return remote(mine, mine, ag_s.at[q, d - 1], ag_r.at[q, d - 1], (r, j * 2 + core))

    def sb_copy(q, d):
        block = ypanel.at[q, panel_rows(lax.rem(chip + m - d, m), core), :]
        return remote(block, block, sb_s.at[q, d], sb_r.at[q, d], (r, sib))

    def xs_copy(q, d):
        j = lax.rem(chip + d, m)
        return remote(
            ypart.at[q, part_rows(j, False), :], xrecv.at[q, d], xs_s.at[q, d], xs_r.at[q, d], (r, sib)
        )

    def load_block(q):
        load_om[q].wait()
        hi, lo = split2(om_in[q])
        om2[q, :, 0:B] = hi
        om2[q, :, B : 2 * B] = lo

    def partial_rows(q, first, end):
        step = 2 * B
        for k in range(first * B // step, end * B // step):
            rows = slice(k * step, (k + 1) * step)
            both = jnp.dot(a_mat[rows, :], om2[q], preferred_element_type=F32)
            ypart[q, rows, :] = both[:, :B] + both[:, B:]

    def partial_sample(q):
        load_block(q)
        partial_rows(q, 0, RB_DEV)

    def swap_partial(q):
        each_chip(lambda d: xs_copy(q, d).start())
        xs_copy(q, 0).start()

    def send_sample(q):
        def step(d):
            xs_copy(q, d).wait_recv()
            ypart[q, part_rows(lax.rem(chip + d, m), True), :] += xrecv[q, d]
            rs_copy(q, d).start()

        each_chip(step)

    def reduce_sample(q):
        xs_copy(q, 0).wait_recv()
        total = ypart[q, part_rows(chip, True), :] + xrecv[q, 0]
        each_chip(lambda d: rs_copy(q, d).wait_recv())
        for d in range(m - 1):
            total = total + rs_recv[q, d]
        ypanel[q, panel_rows(chip, core), :] = total
        each_chip(lambda d: ag_copy(q, d).start())
        sb_copy(q, 0).start()
        y_out[:, lanes(q)] = total

    def swap_sample(q):
        def step(d):
            ag_copy(q, d).wait_recv()
            sb_copy(q, d).start()

        each_chip(step)

    def finish_sample(q):
        sb_copy(q, 0).wait_recv()
        each_chip(lambda d: sb_copy(q, d).wait_recv())
        hi, lo = split2(ypanel[q])
        y2[:, 2 * q * B : (2 * q + 1) * B] = hi
        y2[:, (2 * q + 1) * B : (2 * q + 2) * B] = lo

    def gram_rows(q):
        dims = (((0,), (0,)), ((), ()))
        own = slice(2 * q * B, (2 * q + 2) * B)
        parts = lax.dot_general(y2[:, own], y2[:, : own.stop], dims, preferred_element_type=F32)
        both = parts[:B, :] + parts[B:, :]
        for j in range(q + 1):
            g = both[:, 2 * j * B : (2 * j + 1) * B] + both[:, (2 * j + 1) * B : (2 * j + 2) * B]
            g = g * (1.0 / (RB_DEV * B))
            g_out[0, lanes(q), lanes(j)] = g
            if j < q:
                g_out[0, lanes(j), lanes(q)] = g.T

    def piece(i):
        return slice(i * PIECE, (i + 1) * PIECE)

    def inward(q, i, center):
        dst = zcross if center else zin
        sem = zx_r if center else zc_r
        return remote(
            zpart.at[q, piece(i), :], dst.at[q, piece(i), :], zc_s.at[q, i], sem.at[q, i], (inner, c)
        )

    def outward(q, i):
        part = z_out.at[piece(i), lanes(q)]
        return remote(part, part, zt_s.at[q, i], zt_r.at[q, i], (outer, c))

    def onward(q, i):
        part = z_out.at[piece(i), lanes(q)]
        return remote(part, part, zf_s.at[q, i], zt_r.at[q, i], (outer, c))

    def finish_piece(q, i):
        @pl.when(is_center)
        def _():
            inward(q, i, True).wait_recv()
            z_out[piece(i), lanes(q)] = zpart[q, piece(i), :] + zcross[q, piece(i), :]

            @pl.when(has_outer)
            def _():
                outward(q, i).start()

    def chain_piece(q, i):
        if i % (B // PIECE) == 0:
            rows = lanes(i * PIECE // B)
            both = jnp.dot(a_t[rows, :], y2[:, 2 * q * B : (2 * q + 2) * B], preferred_element_type=F32)
            zpart[q, rows, :] = both[:, :B] + both[:, B:]

        @pl.when(has_outer)
        def _():
            inward(q, i, False).wait_recv()
            zpart[q, piece(i), :] += zin[q, piece(i), :]

        @pl.when(is_center)
        def _():
            inward(q, i, True).start()

        @pl.when(not_center)
        def _():
            inward(q, i, False).start()

    first = RB_DEV // 2 if compact else RB_DEV
    load_block(0)
    place(codes, tiles_f, a_mat, 0, first, CB_DEV, row_code)
    partial_rows(0, 0, first)
    pl.semaphore_wait(barrier, 1 + (m - 1) + (n_rows - 1))
    swap_partial(0)
    place(codes, tiles_f, a_mat, first, RB_DEV, CB_DEV, row_code)
    partial_rows(0, first, RB_DEV)
    partial_sample(1)
    swap_partial(1)
    send_sample(0)
    for s in range(slots):
        tile_t[s] = tiles_f[s].T
    place(codes, tile_t, a_t, 0, CB_DEV, RB_DEV, lambda i, j: j * CB_DEV + i)
    send_sample(1)
    reduce_sample(0)
    partial_sample(2)
    swap_partial(2)
    reduce_sample(1)
    send_sample(2)
    swap_sample(0)
    partial_sample(3)
    swap_partial(3)
    finish_sample(0)

    between = {
        (0, 0): lambda: send_sample(3),
        (0, 1): lambda: reduce_sample(2),
        (0, 3): lambda: swap_sample(1),
        (0, 5): lambda: reduce_sample(3),
        (0, 7): lambda: finish_sample(1),
        (1, 1): lambda: gram_rows(0),
        (1, 2): lambda: swap_sample(2),
        (1, 5): lambda: gram_rows(1),
        (1, 7): lambda: finish_sample(2),
        (2, 1): lambda: swap_sample(3),
        (2, 5): lambda: gram_rows(2),
        (2, 7): lambda: finish_sample(3),
    }
    late = []
    for q in range(chunks):
        for i in range(pieces):
            chain_piece(q, i)
            late.append((q, i))
            if len(late) > LAG:
                finish_piece(*late.pop(0))
            if (q, i) in between:
                between[q, i]()
    for item in late:
        finish_piece(*item)
    gram_rows(3)

    for q in range(chunks):
        for i in range(pieces):

            @pl.when(not_center)
            def _():
                outward(q, i).wait_recv()

            if n_rows > 4:

                @pl.when(jnp.logical_and(has_outer, not_center))
                def _():
                    onward(q, i).start()

    for q in range(chunks):
        xs_copy(q, 0).wait_send()
        each_chip(lambda d: xs_copy(q, d).wait_send())
        each_chip(lambda d: rs_copy(q, d).wait_send())
        each_chip(lambda d: ag_copy(q, d).wait_send())
        sb_copy(q, 0).wait_send()
        each_chip(lambda d: sb_copy(q, d).wait_send())
        for i in range(pieces):
            inward(q, i, True).wait_send()

            @pl.when(jnp.logical_and(is_center, has_outer))
            def _():
                outward(q, i).wait_send()

            if n_rows > 4:

                @pl.when(jnp.logical_and(has_outer, not_center))
                def _():
                    onward(q, i).wait_send()


def solution(mesh):
    n_rows, n_cols = mesh.shape["rows"], mesh.shape["cols"]

    def local(tile_values, tile_rows, tile_cols, live_counts, test_block):
        slots = tile_values.shape[2]
        test_cols = test_block.shape[1]
        m = n_cols // 2
        panel, ctx = RB_DEV * B, CB_DEV * B
        chunks = test_cols // B
        pieces = ctx // PIECE
        share = panel // n_cols
        vmem = pl.BlockSpec(memory_space=pltpu.VMEM)
        smem = pl.BlockSpec(memory_space=pltpu.SMEM)
        hbm = pl.BlockSpec(memory_space=pltpu.HBM)
        dma = pltpu.SemaphoreType.DMA
        return pl.pallas_call(
            functools.partial(kernel, n_rows, n_cols, slots),
            out_shape=(
                jax.ShapeDtypeStruct((panel // n_cols, test_cols), F32),
                jax.ShapeDtypeStruct((ctx, test_cols), F32),
                jax.ShapeDtypeStruct((1, test_cols, test_cols), F32),
            ),
            in_specs=[smem, smem, smem, hbm, hbm],
            out_specs=(vmem, vmem, vmem),
            scratch_shapes=[
                pltpu.VMEM((slots, 8, B), jnp.int32),
                pltpu.VMEM((slots, B, B), BF16),
                pltpu.VMEM((slots, B, B), F32),
                pltpu.VMEM((slots, B, B), F32),
                pltpu.VMEM((chunks, ctx, B), F32),
                pltpu.VMEM((chunks, ctx, 2 * B), BF16),
                pltpu.VMEM((panel, ctx), BF16),
                pltpu.VMEM((ctx, panel), BF16),
                pltpu.VMEM((chunks, panel, B), F32),
                pltpu.VMEM((chunks, m, share, B), F32),
                pltpu.VMEM((chunks, m - 1, share, B), F32),
                pltpu.VMEM((chunks, panel, B), F32),
                pltpu.VMEM((panel, 2 * test_cols), BF16),
                pltpu.VMEM((chunks, ctx, B), F32),
                pltpu.VMEM((chunks, ctx, B), F32),
                pltpu.VMEM((chunks, ctx, B), F32),
                dma((1 + chunks,)),
                dma((chunks, m)), dma((chunks, m)),
                dma((chunks, m - 1)), dma((chunks, m - 1)),
                dma((chunks, m - 1)), dma((chunks, m - 1)),
                dma((chunks, m)), dma((chunks, m)),
                dma((chunks, pieces)), dma((chunks, pieces)), dma((chunks, pieces)),
                dma((chunks, pieces)), dma((chunks, pieces)), dma((chunks, pieces)),
            ],
            compiler_params=pltpu.CompilerParams(
                collective_id=0, has_side_effects=True, vmem_limit_bytes=51 * 1024 * 1024
            ),
            cost_estimate=pl.CostEstimate(flops=4_000_000_000, bytes_accessed=4_000_000, transcendentals=0),
        )(tile_rows, tile_cols, live_counts, tile_values, test_block)

    return jax.shard_map(
        local,
        mesh=mesh,
        in_specs=(
            P("rows", "cols", None, None, None),
            P("rows", "cols", None),
            P("rows", "cols", None),
            P("rows", "cols"),
            P("cols", None),
        ),
        out_specs=(P(("rows", "cols"), None), P("cols", None), P("rows", None, None)),
        check_vma=False,
    )
```
